32 devices in a mesh: dp: 4 (over x, core), tensor: 8 (over z, y).
Axes of the slice: x: 2, y: 2, z: 4, core: 2. Of those that a mesh axis runs over, the one named last changes fastest.
Arguments:
- tokens: bfloat16 [2, 12288, 1024], P(None, ('dp', 'tensor')), may hold values from -6 to 6
- segment_ids: int32 [2, 4, 3072], P(None, 'dp'), may hold values from 0 to 3, never falling along the last dimension, each value on 1 to 1370 neighbouring positions
- out_grad: bfloat16 [2, 12288, 1024], P(None, ('dp', 'tensor')), may hold values from -6 to 6
- norm1_gain: bfloat16 [1024], P('dp'), may hold values from 0.25 to 1.75
- norm1_bias: bfloat16 [1024], P('dp'), may hold values from -3 to 3
- qkv_weight: bfloat16 [3, 1024, 1024], P(None, 'dp', 'tensor'), may hold values from -0.25 to 0.25
- qv_bias: bfloat16 [2, 1024], P(None, ('tensor', 'dp')), may hold values from -3 to 3
- proj_weight: bfloat16 [1024, 1024], P('tensor', 'dp'), may hold values from -1 to 1
- proj_bias: bfloat16 [1024], P('dp'), may hold values from -3 to 3
- scale1: bfloat16 [1024], P('dp'), may hold values from 0.25 to 1.75
- norm2_gain: bfloat16 [1024], P('dp'), may hold values from 0.25 to 1.75
- norm2_bias: bfloat16 [1024], P('dp'), may hold values from -3 to 3
- fc1_weight: bfloat16 [1024, 4096], P('dp', 'tensor'), may hold values from -0.1875 to 0.1875
- fc1_bias: bfloat16 [4096], P(('tensor', 'dp')), may hold values from -3 to 3
- fc2_weight: bfloat16 [4096, 1024], P('tensor', 'dp'), may hold values from -0.09375 to 0.09375
- fc2_bias: bfloat16 [1024], P('dp'), may hold values from -3 to 3
- scale2: bfloat16 [1024], P('dp'), may hold values from 0.25 to 1.75
Outputs:
- block_out: bfloat16 [2, 12288, 1024], P(None, ('dp', 'tensor'))
- tokens_grad: bfloat16 [2, 12288, 1024], P(None, ('dp', 'tensor'))
- grad_norm1_gain: float32 [1024], P('dp')
- grad_norm1_bias: float32 [1024], P('dp')
- grad_qkv_weight: float32 [3, 1024, 1024], P(None, 'dp', 'tensor')
- grad_qv_bias: float32 [2, 1024], P(None, ('tensor', 'dp'))
- grad_proj_weight: float32 [1024, 1024], P('tensor', 'dp')
- grad_proj_bias: float32 [1024], P('dp')
- grad_scale1: float32 [1024], P('dp')
- grad_norm2_gain: float32 [1024], P('dp')
- grad_norm2_bias: float32 [1024], P('dp')
- grad_fc1_weight: float32 [1024, 4096], P('dp', 'tensor')
- grad_fc1_bias: float32 [4096], P(('tensor', 'dp'))
- grad_fc2_weight: float32 [4096, 1024], P('tensor', 'dp')
- grad_fc2_bias: float32 [1024], P('dp')
- grad_scale2: float32 [1024], P('dp')
The draws below stay inside these ranges and needn't reach their ends.
Inputs may be any that keep to these rules, and one draw needn't show every extreme that they name: `segment_ids`: along each run the image number never falls; each image is a run of 1 to 1370 tokens, and some image has exactly 1370.
All inputs are finite; a program needn't handle non-finite values.
Results may differ from the reference program's by a relative error of at most 0.023.
Values may be sent and summed in bfloat16 or wider, within the bound.
A program may use at most 192 MiB of HBM per device.

```python
import math
from functools import partial
import jax
import jax.numpy as jnp
import numpy as np
from jax import lax

D = 1024
HEADS = 16
HEAD_DIM = 64
FF = 4096
IMG_MAX = 1370
TOK_DEV = 3072
MB = 2
MB_TOK = 12288
IMAGES = 4
N_DP = 4


def block_scale(rng, shape, split, smallest, top_value):
    level, own = 1.0, jax.random.fold_in(rng, 6)
    for position, parts in split:
        draws = jnp.exp(jax.random.uniform(jax.random.fold_in(own, position), (parts,), jnp.float32, smallest / len(split), top_value / len(split)))
        level = level * jnp.repeat(draws, shape[position] // parts).reshape([-1 if axis == position else 1 for axis in range(len(shape))])
    return level


def length_profile(amount, total, reach, lean):
    portions = [(1 << 20) // math.isqrt(standing ** lean) + 1 for standing in range(2, amount + 1)]
    surplus, holding = total - reach - (amount - 1), [1] * (amount - 1)
    while surplus > 0:
        candidates = [i for i in range(amount - 1) if holding[i] < reach]
        pool, left = sum([portions[i] for i in candidates]), surplus
        for i in candidates:
            more = min(reach - holding[i], max(1, left * portions[i] // pool), surplus)
            holding[i] = holding[i] + more
            surplus = surplus - more
    return np.array([reach] + holding)


def ragged(key, number_of, total, bound, slope):
    if number_of == 2:
        one = jax.random.randint(key, (), max(1, total - bound), min(bound, total - 1) + 1)
        return jnp.stack([one, total - one])
    lengths = jnp.asarray(length_profile(number_of, total, bound, slope), jnp.int32)
    twos = (number_of - 1) // 2
    donor, sink = lengths[1:1 + 2 * twos:2], lengths[2:2 + 2 * twos:2]
    margin = jnp.minimum(donor - 1, bound - sink)
    shifted = jax.random.randint(jax.random.fold_in(key, 1), (twos,), 0, 1 << 20) % (margin + 1)
    lengths = lengths.at[1:1 + 2 * twos:2].set(donor - shifted).at[2:2 + 2 * twos:2].set(sink + shifted)
    return lengths[jax.random.permutation(jax.random.fold_in(key, 2), number_of)]


def normal_values(stream_key, extent, scale, most, shards=(), held_as=jnp.bfloat16):
    level = block_scale(stream_key, extent, shards, -0.22, 0.18) if shards else 1.0
    values = jax.random.normal(stream_key, extent, jnp.float32) * scale * level
    return jnp.minimum(jnp.maximum(values, -most), most).astype(held_as)


def setup_inputs(seed: int = 0) -> dict:
    keys = jax.random.split(jax.random.key(seed), 18)
    tokens = normal_values(keys[0], (MB, MB_TOK, D), 1.0, 6.0, ((1, 32),))
    segment_ids = jax.vmap(lambda own: jnp.searchsorted(jnp.cumsum(ragged(own, IMAGES, TOK_DEV, IMG_MAX, 1)), jnp.arange(TOK_DEV), side="right"))(jax.random.split(keys[1], MB * N_DP)).reshape((MB, N_DP, TOK_DEV)).astype(jnp.int32)
    out_grad = normal_values(keys[2], (MB, MB_TOK, D), 1.0, 6.0, ((1, 32),))
    norm1_gain = jnp.clip(1.0 + 0.15 * jax.random.normal(keys[3], (D,), jnp.float32), 0.25, 1.75).astype(jnp.bfloat16)
    norm1_bias = normal_values(keys[4], (D,), 0.5, 3.0, ((0, 4),))
    qkv_weight = normal_values(keys[5], (3, D, D), (D // 2) ** -0.5, 0.25, ((1, 4), (2, 8)))
    qv_bias = normal_values(keys[6], (2, D), 0.5, 3.0, ((1, 32),))
    proj_weight = normal_values(keys[7], (D, D), (D // 32) ** -0.5, 1.0, ((0, 8), (1, 4)))
    proj_bias = normal_values(keys[8], (D,), 0.5, 3.0, ((0, 4),))
    scale1 = jnp.clip(1.0 + 0.15 * jax.random.normal(keys[9], (D,), jnp.float32), 0.25, 1.75).astype(jnp.bfloat16)
    norm2_gain = jnp.clip(1.0 + 0.15 * jax.random.normal(keys[10], (D,), jnp.float32), 0.25, 1.75).astype(jnp.bfloat16)
    norm2_bias = normal_values(keys[11], (D,), 0.5, 3.0, ((0, 4),))
    fc1_weight = normal_values(keys[12], (D, FF), D ** -0.5, 0.1875, ((0, 4), (1, 8)))
    fc1_bias = normal_values(keys[13], (FF,), 0.5, 3.0, ((0, 32),))
    fc2_weight = normal_values(keys[14], (FF, D), FF ** -0.5, 0.09375, ((0, 8), (1, 4)))
    fc2_bias = normal_values(keys[15], (D,), 0.5, 3.0, ((0, 4),))
    scale2 = jnp.clip(1.0 + 0.15 * jax.random.normal(keys[16], (D,), jnp.float32), 0.25, 1.75).astype(jnp.bfloat16)
    return dict(tokens=tokens, segment_ids=segment_ids, out_grad=out_grad, norm1_gain=norm1_gain, norm1_bias=norm1_bias, qkv_weight=qkv_weight, qv_bias=qv_bias, proj_weight=proj_weight, proj_bias=proj_bias, scale1=scale1, norm2_gain=norm2_gain, norm2_bias=norm2_bias, fc1_weight=fc1_weight, fc1_bias=fc1_bias, fc2_weight=fc2_weight, fc2_bias=fc2_bias, scale2=scale2)


norm_eps = 1e-06
mask_fill = -1e+30
highest = lax.Precision.HIGHEST

@jax.custom_vjp
def low(v):
    return lax.optimization_barrier(v.astype(jnp.bfloat16)).astype(jnp.float32)

@jax.custom_vjp
def low_back(v):
    return v

def low_keep(v):
    return (low(v), None)

def low_pass(kept, grad):
    return (grad,)

def back_keep(v):
    return (v, None)

def back_low(kept, grad):
    return (low(grad),)
low.defvjp(low_keep, low_pass)
low_back.defvjp(back_keep, back_low)

def layer_norm(values, scale_gain, shift_bias):
    center = values - lax.optimization_barrier(jnp.mean(values, axis=-1, keepdims=True))
    spread = lax.optimization_barrier(jnp.mean(center * center, axis=-1, keepdims=True))
    return center * lax.rsqrt(spread + norm_eps) * scale_gain + shift_bias

def matmul(left, right):
    return jnp.dot(left, right, precision=highest, preferred_element_type=jnp.float32)

def attention(queries, keys_all, values_all, image_ids):
    block_rows = min(512, TOK_DEV)
    run_shape = (N_DP, TOK_DEV, HEADS, HEAD_DIM)

    def one_run(run_inputs):
        run_queries, run_keys, run_values, run_ids = run_inputs

        def one_block(block_id):
            row_start = (block_id * block_rows).astype(jnp.int32)
            query_block = lax.dynamic_slice_in_dim(run_queries, row_start, block_rows, 0)
            query_ids = lax.dynamic_slice_in_dim(run_ids, row_start, block_rows, 0)
            same_image = query_ids[:, None] == run_ids[None, :]
            scores = low_back(jnp.einsum('qhd,khd->hqk', query_block, run_keys, precision=highest))
            scores = jnp.where(same_image[None], scores, mask_fill)
            weights_p = low(jax.nn.softmax(scores, axis=-1))
            return jnp.einsum('hqk,khd->qhd', weights_p, run_values, precision=highest)
        blocks = lax.map(jax.checkpoint(one_block), jnp.arange(TOK_DEV // block_rows, dtype=jnp.int32))
        return blocks.reshape(TOK_DEV, HEADS, HEAD_DIM)
    runs = lax.map(one_run, (queries.reshape(run_shape), keys_all.reshape(run_shape), values_all.reshape(run_shape), image_ids))
    return runs.reshape(N_DP * TOK_DEV, HEADS * HEAD_DIM)

def forward(params, rows_in, image_ids):
    norm1_gain, norm1_bias, qkv_weight, qv_bias, proj_weight, proj_bias, scale1, norm2_gain, norm2_bias, fc1_weight, fc1_bias, fc2_weight, fc2_bias, scale2 = params
    normed_one = low(layer_norm(rows_in, norm1_gain, norm1_bias))
    queries = low(low_back((matmul(normed_one, qkv_weight[0]) + qv_bias[0]) * 0.125))
    keys_all = low(low_back(matmul(normed_one, qkv_weight[1])))
    values_all = low(low_back(matmul(normed_one, qkv_weight[2]) + qv_bias[1]))
    attended = attention(queries, keys_all, values_all, image_ids)
    attended = low(low_back(attended))
    branch_one = low_back(matmul(attended, proj_weight) + proj_bias)
    middle = rows_in + scale1 * branch_one
    normed_two = low(layer_norm(middle, norm2_gain, norm2_bias))
    pre_act = low_back(matmul(normed_two, fc1_weight) + fc1_bias)
    activated = low(jax.nn.gelu(pre_act, approximate=False))
    branch_two = low_back(matmul(activated, fc2_weight) + fc2_bias)
    return middle + scale2 * branch_two

def reference(tokens, segment_ids, out_grad, norm1_gain, norm1_bias, qkv_weight, qv_bias, proj_weight, proj_bias, scale1, norm2_gain, norm2_bias, fc1_weight, fc1_bias, fc2_weight, fc2_bias, scale2):
    params = tuple((param_arr.astype(jnp.float32) for param_arr in (norm1_gain, norm1_bias, qkv_weight, qv_bias, proj_weight, proj_bias, scale1, norm2_gain, norm2_bias, fc1_weight, fc1_bias, fc2_weight, fc2_bias, scale2)))
    gradients = tuple((jnp.zeros_like(param_arr) for param_arr in params))
    outputs = []
    input_grads = []
    for micro in range(MB):
        rows_in = tokens[micro].astype(jnp.float32)
        result, pullback = jax.vjp(partial(forward, image_ids=segment_ids[micro]), params, rows_in)
        param_grads, rows_grad = pullback(out_grad[micro].astype(jnp.float32))
        gradients = jax.tree.map(jnp.add, gradients, param_grads)
        outputs.append(result.astype(jnp.bfloat16))
        input_grads.append(rows_grad.astype(jnp.bfloat16))
    return (jnp.stack(outputs), jnp.stack(input_grads), gradients[0], gradients[1], gradients[2], gradients[3], gradients[4], gradients[5], gradients[6], gradients[7], gradients[8], gradients[9], gradients[10], gradients[11], gradients[12], gradients[13])
```

```python
import jax
import jax.numpy as jnp
from jax import lax
from jax.experimental import pallas as pl
from jax.experimental.pallas import tpu as pltpu
from jax.sharding import Mesh, PartitionSpec as P

HEAD_DIM = 64

norm_eps = 1e-06
mask_fill = -1e30
query_rows = 512
key_rows = 512
contract_rows = (((0,), (0,)), ((), ()))
contract_cols = (((1,), (1,)), ((), ()))
everywhere = ("o", "c", "a", "r")


def dot_f32(left, right, dims=(((1,), (0,)), ((), ()))):
    return lax.dot_general(left, right, dims, preferred_element_type=jnp.float32)


def norm_parts(values):
    center = values - jnp.mean(values, axis=-1, keepdims=True)
    rate = lax.rsqrt(jnp.mean(center * center, axis=-1, keepdims=True) + norm_eps)
    return center * rate, rate


def norm_back(normed, rate, gain, grad):
    scaled = gain * grad
    average = jnp.mean(scaled, axis=-1, keepdims=True)
    along = jnp.mean(scaled * normed, axis=-1, keepdims=True)
    return rate * (scaled - average - normed * along)


def head_part(rows, head):
    lane = lax.broadcasted_iota(jnp.int32, rows.shape, 1)
    return jnp.where(lane // HEAD_DIM == head, rows, jnp.zeros_like(rows))


def forward_kernel(low_ref, high_ref, q_ref, k_ref, v_ref, idq_ref, idk_ref, out_ref, lse_ref):
    block = pl.program_id(1)
    queries = q_ref[...]
    heads = queries.shape[1] // HEAD_DIM
    rows = queries.shape[0]
    parts = [head_part(queries, head) for head in range(heads)]
    ids_query = idq_ref[...]

    def step(index, carry):
        start = pl.multiple_of(index * key_rows, key_rows)
        keys = k_ref[pl.ds(start, key_rows), :]
        values = v_ref[pl.ds(start, key_rows), :].T
        same = idk_ref[pl.ds(start, key_rows), :] == ids_query
        result = []
        for head in range(heads):
            top, total, acc = carry[head]
            scores = jnp.where(same, dot_f32(keys, parts[head], contract_cols), mask_fill)
            new_top = jnp.maximum(top, jnp.max(scores, axis=0, keepdims=True))
            expon = jnp.exp(scores - new_top)
            shrink = jnp.exp(top - new_top)
            total = shrink * total + jnp.sum(expon, axis=0, keepdims=True)
            mine = values[head * HEAD_DIM : (head + 1) * HEAD_DIM]
            acc = shrink * acc + dot_f32(mine, expon.astype(jnp.bfloat16))
            result.append((new_top, total, acc))
        return tuple(result)

    start_carry = tuple(
        (
            jnp.full((1, rows), mask_fill, jnp.float32),
            jnp.zeros((1, rows), jnp.float32),
            jnp.zeros((HEAD_DIM, rows), jnp.float32),
        )
        for _ in range(heads)
    )
    final = lax.fori_loop(low_ref[block], high_ref[block], step, start_carry)
    merged = jnp.concatenate([acc / total for _, total, acc in final], axis=0)
    out_ref[...] = merged.T.astype(out_ref.dtype)
    lse_ref[0, 0] = jnp.concatenate([top + jnp.log(total) for top, total, _ in final], axis=0)


def backward_kernel(
    low_ref, high_ref, q_ref, k_ref, v_ref, idq_ref, idk_ref, att_ref, d_att_ref, lse_ref,
    dq_ref, dk_ref, dv_ref, dk_sum, dv_sum,
):
    block = pl.program_id(1)

    @pl.when(block == 0)
    def _():
        dk_sum[...] = jnp.zeros_like(dk_sum)
        dv_sum[...] = jnp.zeros_like(dv_sum)

    queries, d_att = q_ref[...], d_att_ref[...]
    heads = queries.shape[1] // HEAD_DIM
    rows = queries.shape[0]
    parts = [head_part(queries, head) for head in range(heads)]
    d_parts = [head_part(d_att, head) for head in range(heads)]
    ids_query = idq_ref[...]
    products = (att_ref[...].astype(jnp.float32) * d_att.astype(jnp.float32)).T
    inner = [
        jnp.sum(products[head * HEAD_DIM : (head + 1) * HEAD_DIM], axis=0, keepdims=True)
        for head in range(heads)
    ]
    lse = lse_ref[0, 0]

    def step(index, carry):
        start = pl.multiple_of(index * key_rows, key_rows)
        here = pl.ds(start, key_rows)
        keys, values = k_ref[here, :], v_ref[here, :]
        keys_turned = keys.T
        same = idk_ref[here, :] == ids_query
        result = []
        d_value, d_key = dv_sum[here, :], dk_sum[here, :]
        for head in range(heads):
            scores = jnp.where(same, dot_f32(keys, parts[head], contract_cols), mask_fill)
            probs = jnp.exp(scores - lse[head : head + 1])
            d_probs = dot_f32(values, d_parts[head], contract_cols)
            d_scores = (probs * (d_probs - inner[head])).astype(jnp.bfloat16)
            d_value = d_value + dot_f32(probs.astype(jnp.bfloat16), d_parts[head])
            d_key = d_key + dot_f32(d_scores, parts[head])
            mine = keys_turned[head * HEAD_DIM : (head + 1) * HEAD_DIM]
            result.append(carry[head] + dot_f32(mine, d_scores))
        dv_sum[here, :] = d_value
        dk_sum[here, :] = d_key
        return tuple(result)

    empty = tuple(jnp.zeros((HEAD_DIM, rows), jnp.float32) for _ in range(heads))
    final = lax.fori_loop(low_ref[block], high_ref[block], step, empty)
    dq_ref[...] = (jnp.concatenate(final, axis=0).T * 0.125).astype(dq_ref.dtype)

    @pl.when(block == pl.num_programs(1) - 1)
    def _():
        dk_ref[...] = dk_sum[...].astype(dk_ref.dtype)
        dv_ref[...] = dv_sum[...].astype(dv_ref.dtype)


def column_specs(tok_count, col_blocks, group=0):
    q_spec = pl.BlockSpec((query_rows, 128), lambda g, i, *_: (i, group + g))
    k_spec = pl.BlockSpec((tok_count, 128), lambda g, i, *_: (0, col_blocks + group + g))
    v_spec = pl.BlockSpec((tok_count, 128), lambda g, i, *_: (0, 2 * col_blocks + group + g))
    idq_spec = pl.BlockSpec((1, query_rows), lambda g, i, *_: (0, i))
    idk_spec = pl.BlockSpec((tok_count, 1), lambda g, i, *_: (0, 0))
    lse_spec = pl.BlockSpec(
        (1, 1, 128 // HEAD_DIM, query_rows), lambda g, i, *_: (group + g, i, 0, 0)
    )
    return q_spec, k_spec, v_spec, idq_spec, idk_spec, lse_spec


def attention(qkv, bounds, ids_row, ids_col):
    tok_count, cols3 = qkv.shape
    cols = cols3 // 3
    blocks, groups = tok_count // query_rows, cols // 128
    q_spec, k_spec, v_spec, idq_spec, idk_spec, lse_spec = column_specs(tok_count, groups)
    pairs = tok_count * tok_count // 2
    return pl.pallas_call(
        forward_kernel,
        grid_spec=pltpu.PrefetchScalarGridSpec(
            num_scalar_prefetch=2,
            grid=(groups, blocks),
            in_specs=[q_spec, k_spec, v_spec, idq_spec, idk_spec],
            out_specs=[q_spec, lse_spec],
        ),
        out_shape=[
            jax.ShapeDtypeStruct((tok_count, cols), jnp.bfloat16),
            jax.ShapeDtypeStruct((groups, blocks, 128 // HEAD_DIM, query_rows), jnp.float32),
        ],
        compiler_params=pltpu.CompilerParams(vmem_limit_bytes=40 * 1024 * 1024),
        cost_estimate=pl.CostEstimate(
            flops=pairs * 32 * cols, bytes_accessed=2 * qkv.size, transcendentals=2 * pairs
        ),
    )(*bounds, qkv, qkv, qkv, ids_row, ids_col)


def attention_back(qkv, bounds, ids_row, ids_col, att, d_att, lse, group):
    tok_count, cols3 = qkv.shape
    cols = cols3 // 3
    blocks, groups = tok_count // query_rows, cols // 128
    q_spec, k_spec, v_spec, idq_spec, idk_spec, lse_spec = column_specs(tok_count, groups, group)
    pairs = tok_count * tok_count // 2
    out_spec = pl.BlockSpec((query_rows, 128), lambda g, i, *_: (i, 0))
    out_whole = pl.BlockSpec((tok_count, 128), lambda g, i, *_: (0, 0))
    one = jax.ShapeDtypeStruct((tok_count, 128), jnp.bfloat16)
    return pl.pallas_call(
        backward_kernel,
        grid_spec=pltpu.PrefetchScalarGridSpec(
            num_scalar_prefetch=2,
            grid=(1, blocks),
            in_specs=[q_spec, k_spec, v_spec, idq_spec, idk_spec, q_spec, q_spec, lse_spec],
            out_specs=[out_spec, out_whole, out_whole],
            scratch_shapes=[
                pltpu.VMEM((tok_count, 128), jnp.float32),
                pltpu.VMEM((tok_count, 128), jnp.float32),
            ],
        ),
        out_shape=[one, one, one],
        compiler_params=pltpu.CompilerParams(vmem_limit_bytes=48 * 1024 * 1024),
        cost_estimate=pl.CostEstimate(
            flops=pairs * 40 * 128, bytes_accessed=4 * qkv.size, transcendentals=2 * pairs
        ),
    )(*bounds, qkv, qkv, qkv, ids_row, ids_col, att, d_att, lse)


pieces = 2


def entry_kernel(
    outer_count, rest_count, tok_ref, w_in_ref, pack_ref, ids_ref, x_ref, w_ref, packs_ref, ids_out_ref,
    ids_send, ids_recv, ids_sem,
    pack_sem, pack_send, pack_recv, packs_send, packs_recv, move_send, move_recv, rest_send, rest_recv, core_send, core_recv,
    w_send, w_recv, outer_send, outer_recv, own_sem,
):
    o, c, a, r = (lax.axis_index(name) for name in everywhere)
    rows = tok_ref.shape[1]
    part = rows // pieces
    w_rows = w_in_ref.shape[1]
    half, low = a // 2, a % 2
    counts = (outer_count, 2, 4, rest_count)
    here_spot = (o, c, a, r)
    dp_shifts = [(i, j, 0, 0) for i in range(outer_count) for j in range(2)][1:]
    tensor_shifts = [(0, 0, i, j) for i in range(4) for j in range(rest_count)][1:]
    core_shifts = [(0, i, j, 0) for i in range(2) for j in range(4)][1:]

    def away(shift):
        return tuple((spot + s) % n for spot, s, n in zip(here_spot, shift, counts))

    def back(shift):
        return tuple((spot - s + n) % n for spot, s, n in zip(here_spot, shift, counts))

    partners = [away(shift) for shift in sorted({*dp_shifts, *tensor_shifts, *core_shifts})]
    barrier = pltpu.get_barrier_semaphore()
    for partner in partners:
        pl.semaphore_signal(barrier, inc=1, device_id=partner, device_id_type=pl.DeviceIdType.MESH)
    pl.semaphore_wait(barrier, len(partners))
    peer = (o, 1 - c, a, r)

    def remote(src, dst, send, recv, target):
        return pltpu.make_async_remote_copy(
            src_ref=src, dst_ref=dst, send_sem=send, recv_sem=recv,
            device_id=target, device_id_type=pl.DeviceIdType.MESH,
        )

    def pack_spot(spot):
        return packs_ref.at[spot[2] * rest_count + spot[3], spot[0] * 2 + spot[1]]

    def pack_group(spot):
        return packs_ref.at[spot[2] * rest_count + spot[3]]

    def pack_copy(i):
        return remote(
            pack_ref, pack_spot(here_spot), pack_send.at[i], pack_recv.at[i], away(dp_shifts[i])
        )

    def packs_copy(i):
        mine = pack_group(here_spot)
        return remote(mine, mine, packs_send.at[i], packs_recv.at[i], away(tensor_shifts[i]))

    pack_own = pltpu.make_async_copy(pack_ref, pack_spot(here_spot), pack_sem)
    pack_own.start()
    ids_own = pltpu.make_async_copy(ids_ref, ids_out_ref.at[c], ids_sem)
    ids_own.start()
    ids_copy = remote(ids_ref, ids_out_ref.at[c], ids_send, ids_recv, peer)
    ids_copy.start()
    for i in range(len(dp_shifts)):
        pack_copy(i).start()

    def x_rows(seq_spot, rest_spot, piece):
        start = (seq_spot * rest_count + rest_spot) * rows + piece * part
        return x_ref.at[pl.ds(pl.multiple_of(start, part), part), :]

    def tok_rows(batch, piece):
        return tok_ref.at[batch, pl.ds(piece * part, part), :]

    def own_copy(batch, piece):
        return pltpu.make_async_copy(
            tok_rows(batch, piece), x_rows(a, r, piece), own_sem.at[piece]
        )

    def move_copy(batch, piece):
        return remote(
            tok_rows(batch, piece), x_rows(a, r, piece),
            move_send.at[batch, piece], move_recv.at[low, piece], (o, half, 2 * batch + c, r),
        )

    def stays(batch):
        return jnp.logical_and(half == c, 2 * batch + c == a)

    for piece in range(pieces):
        for batch in range(2):
            @pl.when(stays(batch))
            def _():
                own_copy(batch, piece).start()

            @pl.when(jnp.logical_not(stays(batch)))
            def _():
                move_copy(batch, piece).start()

    def w_spot(outer_spot, core_spot, turn):
        start = pl.multiple_of((outer_spot * 2 + core_spot) * w_rows, w_rows)
        return w_ref.at[turn, :, pl.ds(start, w_rows), :]

    w_own = pltpu.make_async_copy(w_in_ref, w_spot(o, c, low), own_sem.at[pieces])

    def w_copy(target):
        return remote(
            w_in_ref, w_spot(o, c, low), w_send.at[target], w_recv.at[c, low], (o, half, target, r)
        )

    for target in range(4):
        same = jnp.logical_and(half == c, a == target)

        @pl.when(same)
        def _():
            w_own.start()

        @pl.when(jnp.logical_not(same))
        def _():
            w_copy(target).start()

    pack_own.wait()
    for i, shift in enumerate(dp_shifts):
        spot = pack_spot(back(shift))
        remote(spot, spot, pack_send.at[i], pack_recv.at[i], peer).wait_recv()
    for i in range(len(tensor_shifts)):
        packs_copy(i).start()

    def rest_copy(turn, piece, shift):
        here = x_rows(2 * c + turn, r, piece)
        return remote(
            here, here, rest_send.at[turn, piece, shift - 1], rest_recv.at[turn, piece, shift - 1],
            (o, c, a, (r + shift) % rest_count),
        )

    def rest_landed(turn, piece, shift):
        here = x_rows(2 * c + turn, (r - shift + rest_count) % rest_count, piece)
        return remote(
            here, here, rest_send.at[turn, piece, shift - 1], rest_recv.at[turn, piece, shift - 1],
            peer,
        )

    def core_copy(turn, piece, shift, core):
        here = x_rows(2 * core + turn, (r - shift + rest_count) % rest_count, piece)
        return remote(
            here, here, core_send.at[turn, piece, shift], core_recv.at[turn, piece, shift], peer
        )

    for piece in range(pieces):
        for turn in range(2):
            same = jnp.logical_and(low == c, 2 * c + turn == a)

            @pl.when(same)
            def _():
                own_copy(0, piece).wait()

            @pl.when(jnp.logical_not(same))
            def _():
                here = x_rows(2 * c + turn, r, piece)
                remote(
                    here, here, move_send.at[0, piece], move_recv.at[turn, piece], peer
                ).wait_recv()

            for shift in range(1, rest_count):
                rest_copy(turn, piece, shift).start()
            core_copy(turn, piece, 0, c).start()

    def outer_copy(core, shift, outer_spot):
        start = pl.multiple_of((outer_spot * 2 + core) * w_rows, w_rows)
        here = w_ref.at[:, :, pl.ds(start, w_rows), :]
        return remote(
            here, here, outer_send.at[core, shift - 1], outer_recv.at[core, shift - 1],
            ((o + shift) % outer_count, c, a, r),
        )

    for core in range(2):
        for turn in range(2):
            same = jnp.logical_and(
                half == c, jnp.logical_and(c == core, low == turn)
            )

            @pl.when(same)
            def _():
                w_own.wait()

            @pl.when(jnp.logical_not(same))
            def _():
                here = w_spot(o, core, turn)
                remote(here, here, w_send.at[0], w_recv.at[core, turn], peer).wait_recv()
        for shift in range(1, outer_count):
            outer_copy(core, shift, o).start()

    for piece in range(pieces):
        for turn in range(2):
            for shift in range(1, rest_count):
                rest_landed(turn, piece, shift).wait_recv()
                core_copy(turn, piece, shift, c).start()

    for core in range(2):
        for shift in range(1, outer_count):
            outer_copy(core, shift, (o - shift + outer_count) % outer_count).wait_recv()
    for piece in range(pieces):
        for turn in range(2):
            for shift in range(rest_count):
                core_copy(turn, piece, shift, 1 - c).wait_recv()

    for piece in range(pieces):
        for batch in range(2):
            @pl.when(jnp.logical_not(stays(batch)))
            def _():
                move_copy(batch, piece).wait_send()
        for turn in range(2):
            for shift in range(1, rest_count):
                rest_copy(turn, piece, shift).wait_send()
            for shift in range(rest_count):
                core_copy(turn, piece, shift, c).wait_send()
    for target in range(4):
        @pl.when(jnp.logical_not(jnp.logical_and(half == c, a == target)))
        def _():
            w_copy(target).wait_send()
    for core in range(2):
        for shift in range(1, outer_count):
            outer_copy(core, shift, o).wait_send()
    for i in range(len(dp_shifts)):
        pack_copy(i).wait_send()
    ids_own.wait()
    ids_copy.wait_send()
    remote(ids_ref, ids_out_ref.at[1 - c], ids_send, ids_recv, peer).wait_recv()
    for i, shift in enumerate(tensor_shifts):
        spot = pack_group(back(shift))
        remote(spot, spot, packs_send.at[i], packs_recv.at[i], peer).wait_recv()
        packs_copy(i).wait_send()


def entry(tokens, qkv_weight, pack, ids):
    outer_count, rest_count = lax.axis_size("o"), lax.axis_size("r")
    batches, rows, width = tokens.shape
    dma = pltpu.SemaphoreType.DMA
    wide, narrow = max(rest_count - 1, 1), max(outer_count - 1, 1)
    return pl.pallas_call(
        lambda *refs: entry_kernel(outer_count, rest_count, *refs),
        in_specs=[pl.BlockSpec(memory_space=pl.ANY)] * 4,
        out_specs=[pl.BlockSpec(memory_space=pl.ANY)] * 4,
        out_shape=[
            jax.ShapeDtypeStruct((4 * rest_count * rows, width), tokens.dtype),
            jax.ShapeDtypeStruct(
                (2, qkv_weight.shape[0], width, qkv_weight.shape[2]), qkv_weight.dtype
            ),
            jax.ShapeDtypeStruct((4 * rest_count, 2 * outer_count, *pack.shape), pack.dtype),
            jax.ShapeDtypeStruct((2, *ids.shape), ids.dtype),
        ],
        scratch_shapes=[
            dma(()), dma(()), dma(()),
            dma(()), dma((2 * outer_count - 1,)), dma((2 * outer_count - 1,)),
            dma((4 * rest_count - 1,)), dma((4 * rest_count - 1,)),
            dma((2, pieces)), dma((2, pieces)),
            dma((2, pieces, wide)), dma((2, pieces, wide)),
            dma((2, pieces, rest_count)), dma((2, pieces, rest_count)),
            dma((4,)), dma((2, 2)), dma((2, narrow)), dma((2, narrow)), dma((pieces + 1,)),
        ],
        compiler_params=pltpu.CompilerParams(collective_id=0, has_side_effects=True),
        cost_estimate=pl.CostEstimate(
            flops=0, bytes_accessed=200 * 1024 * 1024, transcendentals=0
        ),
    )(tokens, qkv_weight, pack, ids)


def exit_kernel(
    outer_count, rest_count, sums_ref, own_ref, total_ref, out_ref,
    dp_got, part, tensor_got, dp_send, dp_recv, tensor_send, tensor_recv,
    move_send, move_recv, own_sem,
):
    o, c, a, r = (lax.axis_index(name) for name in everywhere)
    half, low = a // 2, a % 2
    counts = (outer_count, 2, 4, rest_count)
    here_spot = (o, c, a, r)
    dp_shifts = [(i, j, 0, 0) for i in range(outer_count) for j in range(2)][1:]
    tensor_shifts = [(0, 0, i, j) for i in range(4) for j in range(rest_count)][1:]
    core_shifts = [(0, i, j, 0) for i in range(2) for j in range(4)][1:]

    def away(shift):
        return tuple((spot + s) % n for spot, s, n in zip(here_spot, shift, counts))

    partners = [away(shift) for shift in sorted({*dp_shifts, *tensor_shifts, *core_shifts})]
    barrier = pltpu.get_barrier_semaphore()
    for partner in partners:
        pl.semaphore_signal(barrier, inc=1, device_id=partner, device_id_type=pl.DeviceIdType.MESH)
    pl.semaphore_wait(barrier, len(partners))
    peer = (o, 1 - c, a, r)

    def remote(src, dst, send, recv, target):
        return pltpu.make_async_remote_copy(
            src_ref=src, dst_ref=dst, send_sem=send, recv_sem=recv,
            device_id=target, device_id_type=pl.DeviceIdType.MESH,
        )

    def stays(turn):
        return jnp.logical_and(low == c, 2 * c + turn == a)

    def move_copy(turn):
        return remote(
            own_ref.at[turn], out_ref.at[half], move_send.at[turn], move_recv.at[half],
            (o, low, 2 * c + turn, r),
        )

    stay_copy = pltpu.make_async_copy(own_ref.at[low], out_ref.at[half], own_sem)
    for turn in range(2):
        @pl.when(stays(turn))
        def _():
            stay_copy.start()

        @pl.when(jnp.logical_not(stays(turn)))
        def _():
            move_copy(turn).start()

    def dp_copy(i):
        target = away(dp_shifts[i])
        return remote(
            sums_ref.at[target[0] * 2 + target[1]], dp_got.at[i], dp_send.at[i], dp_recv.at[i],
            target,
        )

    for i in range(len(dp_shifts)):
        dp_copy(i).start()
    total = sums_ref[o * 2 + c]
    for i in range(len(dp_shifts)):
        dp_copy(i).wait_recv()
        total = total + dp_got[i]
    part[...] = total

    def tensor_copy(i):
        return remote(
            part, tensor_got.at[i], tensor_send.at[i], tensor_recv.at[i], away(tensor_shifts[i])
        )

    for i in range(len(tensor_shifts)):
        tensor_copy(i).start()
    for i in range(len(tensor_shifts)):
        tensor_copy(i).wait_recv()
        total = total + tensor_got[i]
    total_ref[...] = total

    for batch in range(2):
        same = jnp.logical_and(half == c, 2 * batch + c == a)

        @pl.when(same)
        def _():
            stay_copy.wait()

        @pl.when(jnp.logical_not(same))
        def _():
            spot = out_ref.at[batch]
            remote(spot, spot, move_send.at[0], move_recv.at[batch], peer).wait_recv()
    for turn in range(2):
        @pl.when(jnp.logical_not(stays(turn)))
        def _():
            move_copy(turn).wait_send()
    for i in range(len(dp_shifts)):
        dp_copy(i).wait_send()
    for i in range(len(tensor_shifts)):
        tensor_copy(i).wait_send()


def leave(sums, own):
    outer_count, rest_count = lax.axis_size("o"), lax.axis_size("r")
    dma = pltpu.SemaphoreType.DMA
    few, many = 2 * outer_count - 1, 4 * rest_count - 1
    shape = sums.shape[1:]
    return pl.pallas_call(
        lambda *refs: exit_kernel(outer_count, rest_count, *refs),
        in_specs=[pl.BlockSpec(memory_space=pltpu.VMEM), pl.BlockSpec(memory_space=pl.ANY)],
        out_specs=[pl.BlockSpec(memory_space=pltpu.VMEM), pl.BlockSpec(memory_space=pl.ANY)],
        out_shape=[
            jax.ShapeDtypeStruct(shape, jnp.float32),
            jax.ShapeDtypeStruct(own.shape, own.dtype),
        ],
        scratch_shapes=[
            pltpu.VMEM((few, *shape), jnp.float32), pltpu.VMEM(shape, jnp.float32),
            pltpu.VMEM((many, *shape), jnp.float32),
            dma((few,)), dma((few,)), dma((many,)), dma((many,)), dma((2,)), dma((2,)), dma(()),
        ],
        compiler_params=pltpu.CompilerParams(collective_id=1, has_side_effects=True),
        cost_estimate=pl.CostEstimate(
            flops=0, bytes_accessed=120 * 1024 * 1024, transcendentals=0
        ),
    )(sums, own)


def mlp_kernel(
    h_ref, dm_ref, w1_ref, w2_ref, bias_ref, m_ref, dh_ref, grad1_ref, grad2_ref, dbias_ref,
    h_turned, dm_turned, kept, sent, got, send_sem, got_sem,
):
    o, core, a, r = (lax.axis_index(name) for name in everywhere)
    block = pl.program_id(0)
    count = pl.num_programs(0) - 1
    slot, other = block % 2, (block + 1) % 2
    peer = (o, 1 - core, a, r)

    def to_peer(index, turn):
        return pltpu.make_async_remote_copy(
            src_ref=sent.at[turn], dst_ref=got.at[index],
            send_sem=send_sem.at[turn], recv_sem=got_sem.at[index],
            device_id=peer, device_id_type=pl.DeviceIdType.MESH,
        )

    @pl.when(block == 0)
    def _():
        barrier = pltpu.get_barrier_semaphore()
        pl.semaphore_signal(barrier, inc=1, device_id=peer, device_id_type=pl.DeviceIdType.MESH)
        pl.semaphore_wait(barrier, 1)
        h_turned[...] = h_ref[...].T
        dm_turned[...] = dm_ref[...].T
        m_ref[...] = jnp.zeros_like(m_ref)
        dh_ref[...] = jnp.zeros_like(dh_ref)

    @pl.when(block >= 2)
    def _():
        to_peer(block - 2, slot).wait_send()

    @pl.when(block < count)
    def _():
        dp_count, _, _, rows = w1_ref.shape
        pre, d_act = bias_ref[...], 0.0
        for d in range(dp_count):
            spot = slice(d * rows, (d + 1) * rows)
            pre = pre + dot_f32(h_ref[:, spot], w1_ref[d, 0], contract_cols)
        for d in range(dp_count):
            spot = slice(d * rows, (d + 1) * rows)
            d_act = d_act + dot_f32(dm_ref[:, spot], w2_ref[d, 0], contract_cols)
        spread = 0.5 * (1.0 + lax.erf(pre * 0.7071067811865476))
        act = (pre * spread).astype(jnp.bfloat16)
        slope = spread + pre * jnp.exp(-0.5 * pre * pre) * 0.3989422804014327
        d_pre = (d_act * slope).astype(jnp.bfloat16)
        dbias_ref[...] = jnp.sum(d_pre.astype(jnp.float32), axis=0, keepdims=True)
        for d in range(dp_count):
            spot = slice(d * rows, (d + 1) * rows)
            m_ref[:, spot] += dot_f32(act, w2_ref[d, 0])
            dh_ref[:, spot] += dot_f32(d_pre, w1_ref[d, 0])
        for d in range(dp_count):
            spot = slice(d * rows, (d + 1) * rows)
            grad1 = dot_f32(h_turned[spot, :], d_pre).astype(jnp.bfloat16)
            grad2 = dot_f32(dm_turned[spot, :], act).astype(jnp.bfloat16)

            @pl.when(core == d % 2)
            def _():
                kept[slot, 0, d // 2] = grad1
                kept[slot, 1, d // 2] = grad2

            @pl.when(core != d % 2)
            def _():
                sent[slot, 0, d // 2] = grad1
                sent[slot, 1, d // 2] = grad2

        to_peer(block, slot).start()

    @pl.when(block >= 1)
    def _():
        to_peer(block - 1, other).wait_recv()
        for turn, out_ref in enumerate((grad1_ref, grad2_ref)):
            mine = kept[other, turn].astype(jnp.float32)
            out_ref[0] = (mine + got[block - 1, turn].astype(jnp.float32)).astype(jnp.bfloat16)

    @pl.when(block == count)
    def _():
        to_peer(block - 1, other).wait_send()


def mlp(rows_low, d_branch, weights, hid, bias):
    tokens_here, width = rows_low.shape
    dp_count, tensor_count, _, rows = weights.shape
    outer = dp_count // 2
    whole = pl.BlockSpec((tokens_here, width), lambda t: (0, 0))
    grad_spec = pl.BlockSpec((1, outer, rows, hid), lambda t: (jnp.maximum(t - 1, 0), 0, 0, 0))
    grad = jax.ShapeDtypeStruct((tensor_count, outer, rows, hid), jnp.bfloat16)
    out = jax.ShapeDtypeStruct((tokens_here, width), jnp.float32)
    last = tensor_count - 1
    line = pl.BlockSpec((1, hid), lambda t: (0, jnp.minimum(t, last)))
    w1_spec = pl.BlockSpec((dp_count, 1, hid, rows), lambda t: (0, jnp.minimum(t, last), 0, 0))
    w2_spec = pl.BlockSpec((dp_count, 1, hid, rows), lambda t: (0, jnp.minimum(t, last), 1, 0))
    return pl.pallas_call(
        mlp_kernel,
        grid=(tensor_count + 1,),
        in_specs=[whole, whole, w1_spec, w2_spec, line],
        out_specs=[whole, whole, grad_spec, grad_spec, line],
        out_shape=[
            out, out, grad, grad,
            jax.ShapeDtypeStruct((1, tensor_count * hid), jnp.float32),
        ],
        scratch_shapes=[
            pltpu.VMEM((width, tokens_here), jnp.bfloat16),
            pltpu.VMEM((width, tokens_here), jnp.bfloat16),
            pltpu.VMEM((2, 2, outer, rows, hid), jnp.bfloat16),
            pltpu.VMEM((2, 2, outer, rows, hid), jnp.bfloat16),
            pltpu.VMEM((tensor_count, 2, outer, rows, hid), jnp.bfloat16),
            pltpu.SemaphoreType.DMA((2,)),
            pltpu.SemaphoreType.DMA((tensor_count,)),
        ],
        compiler_params=pltpu.CompilerParams(
            vmem_limit_bytes=60 * 1024 * 1024, collective_id=2, has_side_effects=True
        ),
        cost_estimate=pl.CostEstimate(
            flops=12 * tokens_here * width * tensor_count * hid,
            bytes_accessed=64 * 1024 * 1024,
            transcendentals=2 * tokens_here * tensor_count * hid,
        ),
    )(rows_low, d_branch, weights, weights, bias)


def gather_parts(shard):
    parts = lax.all_gather(shard, everywhere, axis=0, tiled=False)
    return parts.reshape(lax.axis_size("o") * 2, -1, *shard.shape)


def pick(blocks, index):
    return lax.dynamic_index_in_dim(blocks, index, 0, keepdims=False)


def place_shift(step, count):
    return [(spot, (spot + step) % count) for spot in range(count)]


def move_pairs(step):
    pairs = []
    for core in range(2):
        for seq in range(4):
            batch = (seq % 2) ^ step
            pairs.append((core * 4 + seq, (seq // 2) * 4 + 2 * batch + core))
    return pairs


def move_in(both):
    low = lax.axis_index("a") % 2
    batch = lax.axis_index("a") // 2
    got = [
        lax.ppermute(pick(both, low ^ step), ("c", "a"), move_pairs(step)) for step in range(2)
    ]
    return jnp.stack([jnp.where(batch == 0, got[j], got[1 - j]) for j in range(2)])


def move_out(own):
    low = lax.axis_index("a") % 2
    batch = lax.axis_index("a") // 2
    got = [
        lax.ppermute(
            pick(own, batch ^ step), ("c", "a"), [(t, s) for s, t in move_pairs(step)]
        )
        for step in range(2)
    ]
    return jnp.stack([jnp.where(low == 0, got[b], got[1 - b]) for b in range(2)])


def sum_shards(blocks, axis, dim, dtype):
    count, me = blocks.shape[dim], lax.axis_index(axis)

    def block(spot):
        return lax.dynamic_index_in_dim(blocks, spot, dim, keepdims=False)

    got = [
        lax.ppermute(block((me + step) % count), axis, place_shift(step, count))
        for step in range(1, count)
    ]
    total = block(me).astype(jnp.float32)
    for values in got:
        total = total + values.astype(jnp.float32)
    return total.astype(dtype)


def core_sum(own, sent):
    got = lax.ppermute(sent, "c", [(0, 1), (1, 0)])
    total = (own.astype(jnp.float32) + got.astype(jnp.float32)).astype(jnp.bfloat16)
    return total.reshape(4, lax.axis_size("r"), *total.shape[1:])


def body(
    tokens, segment_ids, out_grad, norm1_gain, norm1_bias, qkv_weight, qv_bias, proj_weight,
    proj_bias, scale1, norm2_gain, norm2_bias, fc1_weight, fc1_bias, fc2_weight, fc2_bias, scale2,
):
    o, c, a, r = (lax.axis_index(name) for name in everywhere)
    outer, rest = lax.axis_size("o"), lax.axis_size("r")
    dp_count, tensor_count = outer * 2, 4 * rest
    batches, rows_here, width = tokens.shape
    own_rows = 2 * rows_here
    tok_count = rows_here * tensor_count
    cols_here, shard_rows = qkv_weight.shape[2], qkv_weight.shape[1]
    own_cols = 2 * cols_here
    hidden = fc1_weight.shape[1] * tensor_count
    short, fc1_short = qv_bias.shape[1], fc1_bias.shape[0]

    vectors = jnp.stack(
        [norm1_gain, norm1_bias, proj_bias, scale1, norm2_gain, norm2_bias, fc2_bias, scale2]
    )
    small = jnp.concatenate([qv_bias.reshape(-1), fc1_bias])
    small = jnp.pad(small[None], ((0, 7), (0, shard_rows - small.shape[0])))
    seq_rows, w_parts, packs, ids = entry(
        tokens, qkv_weight, jnp.concatenate([vectors, small]), segment_ids
    )
    seq_rows, out_grad = lax.optimization_barrier((seq_rows, out_grad))
    vecs = jnp.moveaxis(packs[0, :, :8], 0, 1).reshape(8, width).astype(jnp.float32)
    biases = packs[:, :, 8].astype(jnp.float32)
    bias_fc1 = biases[:, :, 2 * short : 2 * short + fc1_short].reshape(hidden)
    bias_qv = biases[:, :, : 2 * short].reshape(2, 2, rest, dp_count, 2, short)
    bias_qv = lax.dynamic_index_in_dim(bias_qv, c, 0, keepdims=False)
    bias_qv = lax.dynamic_index_in_dim(bias_qv, r, 1, keepdims=False)
    bias_qv = jnp.moveaxis(bias_qv, 2, 0).reshape(2, own_cols)
    bias_qkv = jnp.concatenate([bias_qv[0], jnp.zeros_like(bias_qv[0]), bias_qv[1]])
    scale_qkv = jnp.concatenate([jnp.full((own_cols,), 0.125), jnp.ones((2 * own_cols,))])

    run_ids = pick(pick(ids, a % 2), a // 2)[0]
    blocks = tok_count // query_rows
    first = run_ids.reshape(blocks, query_rows)[:, :1]
    last = run_ids.reshape(blocks, query_rows)[:, -1:]
    low = jnp.sum((run_ids[None] < first).astype(jnp.int32), axis=-1) // key_rows
    reach = jnp.sum((run_ids[None] <= last).astype(jnp.int32), axis=-1)
    bounds = (low, (reach + key_rows - 1) // key_rows)
    ids_row, ids_col = run_ids[None, :], run_ids[:, None]

    weights = gather_parts(jnp.concatenate([fc1_weight.T, fc2_weight, proj_weight]))
    w_proj = weights[:, :, 2 * fc2_weight.shape[0] :]
    w_proj = jnp.transpose(w_proj, (1, 2, 0, 3)).reshape(width, width)
    w_qkv = jnp.moveaxis(w_parts, 0, 2).swapaxes(0, 1).reshape(width, 3 * own_cols)

    def own_of(values):
        split = values.reshape(2, 2, rest, rows_here, values.shape[1])
        split = lax.dynamic_index_in_dim(split, c, 0, keepdims=False)
        split = lax.dynamic_index_in_dim(split, r, 1, keepdims=False)
        return split.reshape(own_rows, values.shape[1])

    normed_all, _ = norm_parts(seq_rows.astype(jnp.float32))
    normed_all_low = (normed_all * vecs[0] + vecs[1]).astype(jnp.bfloat16)
    qkv = ((dot_f32(normed_all_low, w_qkv) + bias_qkv) * scale_qkv).astype(jnp.bfloat16)
    grad_moved = move_in(out_grad)
    att_heads, lse = attention(qkv, bounds, ids_row, ids_col)

    rows_in = own_of(seq_rows).astype(jnp.float32)
    normed_one, rate_one = norm_parts(rows_in)
    sent = att_heads.reshape(2, 2, rest, rows_here, own_cols)
    sent = jnp.swapaxes(sent, 1, 2).reshape(2 * rest, own_rows, own_cols)
    attended = lax.all_to_all(sent, ("c", "r"), split_axis=0, concat_axis=0, tiled=True)
    attended = attended.reshape(2, rest, own_rows, 2, cols_here)
    attended = jnp.transpose(attended, (2, 0, 3, 1, 4)).reshape(own_rows, width)
    branch_one = dot_f32(attended, w_proj) + vecs[2]
    middle = rows_in + vecs[3] * branch_one
    normed_two, rate_two = norm_parts(middle)
    mlp_in = (normed_two * vecs[4] + vecs[5]).astype(jnp.bfloat16)
    grad_top = grad_moved.reshape(own_rows, width).astype(jnp.float32)
    d_branch2 = (vecs[7] * grad_top).astype(jnp.bfloat16)
    d_fc2_bias = jnp.sum(d_branch2.astype(jnp.float32), axis=0)
    branch_two, d_normed_two, grad_fc1, grad_fc2, d_fc1_bias = mlp(
        mlp_in, d_branch2, weights, fc2_weight.shape[0], bias_fc1[None]
    )
    branch_two = branch_two + vecs[6]
    block_out = (middle + vecs[7] * branch_two).astype(jnp.bfloat16)
    d_scale2 = jnp.sum(grad_top * branch_two, axis=0)
    d_gain2 = jnp.sum(d_normed_two * normed_two, axis=0)
    d_bias2 = jnp.sum(d_normed_two, axis=0)
    d_middle = grad_top + norm_back(normed_two, rate_two, vecs[4], d_normed_two)
    d_scale1 = jnp.sum(d_middle * branch_one, axis=0)
    d_branch1 = (vecs[3] * d_middle).astype(jnp.bfloat16)
    d_proj_bias = jnp.sum(d_branch1.astype(jnp.float32), axis=0)
    grad_fc1 = sum_shards(grad_fc1.reshape(4, rest, *grad_fc1.shape[1:]), "r", 1, jnp.bfloat16)
    grad_fc2 = sum_shards(grad_fc2.reshape(4, rest, *grad_fc2.shape[1:]), "o", 2, jnp.bfloat16)
    block_out = move_out(block_out.reshape(2, rows_here, width))
    d_attended = dot_f32(d_branch1, w_proj, contract_cols).astype(jnp.bfloat16)
    sent = d_attended.reshape(own_rows, 2, 2, rest, cols_here)
    sent = jnp.transpose(sent, (1, 3, 0, 2, 4)).reshape(2 * rest, own_rows, own_cols)
    d_heads = lax.all_to_all(sent, ("c", "r"), split_axis=0, concat_axis=0, tiled=True)
    d_heads = jnp.swapaxes(d_heads.reshape(2, rest, 2, rows_here, own_cols), 1, 2)
    d_heads = d_heads.reshape(tok_count, own_cols)

    split = d_branch1.reshape(own_rows, outer, 2, shard_rows)

    def proj_grad(which):
        mine = lax.dynamic_index_in_dim(split, which, 2, keepdims=False)
        grad = dot_f32(mine.reshape(own_rows, width // 2), attended, contract_rows)
        grad = grad.astype(jnp.bfloat16).reshape(outer, shard_rows, tensor_count, cols_here)
        return jnp.transpose(grad, (2, 0, 1, 3))

    grad_proj = core_sum(proj_grad(c), proj_grad(1 - c))
    d_heads, grad_fc1, grad_fc2, grad_proj = lax.optimization_barrier(
        (d_heads, grad_fc1, grad_fc2, grad_proj)
    )

    grad_fc1 = sum_shards(grad_fc1, "o", 1, jnp.bfloat16)
    grad_fc2 = sum_shards(grad_fc2, "r", 1, jnp.bfloat16)
    grad_proj = sum_shards(grad_proj, "o", 2, jnp.bfloat16)
    groups = own_cols // 128
    d_parts = []
    for group in range(groups):
        d_parts.append(
            attention_back(qkv, bounds, ids_row, ids_col, att_heads, d_heads, lse, group)
        )
        if group == 0:
            d_parts, d_heads, grad_fc1, grad_fc2, grad_proj = lax.optimization_barrier(
                (d_parts, d_heads, grad_fc1, grad_fc2, grad_proj)
            )
            shard_fc1 = sum_shards(grad_fc1, "a", 0, jnp.float32)
            shard_fc2 = sum_shards(grad_fc2, "a", 0, jnp.float32)
            grad_proj = sum_shards(grad_proj, "r", 1, jnp.bfloat16)
    d_parts, grad_proj = lax.optimization_barrier((d_parts, grad_proj))

    shard_proj = sum_shards(grad_proj, "a", 0, jnp.float32)
    d_qkv = jnp.concatenate([part[i] for i in range(3) for part in d_parts], axis=1)
    d_rows = dot_f32(d_qkv, w_qkv, contract_cols).astype(jnp.bfloat16)
    d_rows = sum_shards(d_rows.reshape(2, 2, rest, rows_here, width), "c", 0, jnp.bfloat16)
    d_w_qkv = dot_f32(normed_all_low, d_qkv, contract_rows).astype(jnp.bfloat16)
    d_bias_qkv = jnp.sum(d_qkv.astype(jnp.float32), axis=0).reshape(3, 2, cols_here)
    d_bias_qv = jnp.stack([d_bias_qkv[0], d_bias_qkv[2]])
    d_rows, d_w_qkv, d_bias_qv = lax.optimization_barrier((d_rows, d_w_qkv, d_bias_qv))

    d_w_qkv = sum_shards(
        d_w_qkv.reshape(outer, 2, shard_rows, 3, 2, cols_here), "o", 0, jnp.bfloat16
    )
    d_normed_one = sum_shards(d_rows, "r", 1, jnp.float32).reshape(own_rows, width)
    d_w_qkv = jnp.transpose(d_w_qkv, (0, 3, 2, 1, 4)).reshape(4, 3, shard_rows, cols_here)
    shard_qkv = 0.0
    for step in range(4):
        pairs = []
        for core in range(2):
            for seq in range(4):
                k = (seq + step) % 4
                pairs.append((core * 4 + seq, (k // 2) * 4 + 2 * core + k % 2))
        got = lax.ppermute(pick(d_w_qkv, (a + step) % 4), ("c", "a"), pairs)
        shard_qkv = shard_qkv + got.astype(jnp.float32)
    d_gain1 = jnp.sum(d_normed_one * normed_one, axis=0)
    d_bias1 = jnp.sum(d_normed_one, axis=0)
    input_grad = d_middle + norm_back(normed_one, rate_one, vecs[0], d_normed_one)
    spread_qv = jnp.zeros((2, 2, 2, rest, cols_here), jnp.float32)
    spread_qv = lax.dynamic_update_slice(
        spread_qv, d_bias_qv[:, None, :, None], (0, c, 0, r, 0)
    )
    lines = [d_gain1, d_bias1, d_proj_bias, d_scale1, d_gain2, d_bias2, d_fc2_bias, d_scale2]
    lines = jnp.stack(lines).reshape(8, dp_count, shard_rows)
    fc1_lines = d_fc1_bias.reshape(tensor_count, dp_count, fc1_short)
    fc1_lines = jnp.swapaxes(fc1_lines, 0, 1).reshape(dp_count, -1, shard_rows)
    qv_lines = spread_qv.reshape(2, tensor_count, dp_count, short)
    qv_lines = jnp.moveaxis(qv_lines, 2, 0).reshape(dp_count, -1, shard_rows)
    sums = jnp.concatenate([jnp.swapaxes(lines, 0, 1), fc1_lines, qv_lines], axis=1)
    sums = jnp.pad(sums, ((0, 0), (0, -sums.shape[1] % 8), (0, 0)))
    vec_sums, input_grad = leave(
        sums, input_grad.astype(jnp.bfloat16).reshape(2, rows_here, width)
    )
    place = a * rest + r
    fc1_rows = fc1_lines.shape[1]
    grad_fc1_bias = vec_sums[8 : 8 + fc1_rows].reshape(tensor_count, fc1_short)
    grad_fc1_bias = pick(grad_fc1_bias, place)
    grad_qv_bias = vec_sums[8 + fc1_rows : 8 + fc1_rows + qv_lines.shape[1]]
    grad_qv_bias = lax.dynamic_index_in_dim(
        grad_qv_bias.reshape(2, tensor_count, short), place, 1, keepdims=False
    )
    return (
        block_out,
        input_grad,
        vec_sums[0],
        vec_sums[1],
        shard_qkv,
        grad_qv_bias,
        shard_proj.T,
        vec_sums[2],
        vec_sums[3],
        vec_sums[4],
        vec_sums[5],
        shard_fc1,
        grad_fc1_bias,
        shard_fc2.T,
        vec_sums[6],
        vec_sums[7],
    )


def solution(mesh):
    dp, tensor = ("o", "c"), ("a", "r")
    dp_count, tensor_count = mesh.devices.shape
    finer = Mesh(mesh.devices.reshape(dp_count // 2, 2, 4, tensor_count // 4), everywhere)
    rows = P(None, everywhere, None)
    vec = P(dp)
    in_specs = (
        rows, P(None, dp, None), rows, vec, vec, P(None, dp, tensor), P(None, tensor + dp),
        P(tensor, dp), vec, vec, vec, vec, P(dp, tensor), P(tensor + dp), P(tensor, dp), vec, vec,
    )
    out_specs = (
        rows, rows, vec, vec, P(None, dp, tensor), P(None, tensor + dp), P(tensor, dp), vec, vec,
        vec, vec, P(dp, tensor), P(tensor + dp), P(tensor, dp), vec, vec,
    )
    return jax.shard_map(body, mesh=finer, in_specs=in_specs, out_specs=out_specs, check_vma=False)
```

```python
import jax
import jax.numpy as jnp
from jax import lax
from jax.experimental import pallas as pl
from jax.experimental.pallas import tpu as pltpu
from jax.sharding import Mesh, PartitionSpec as P

HEAD_DIM = 64

norm_eps = 1e-06
mask_fill = -1e30
query_rows = 512
key_rows = 512
contract_rows = (((0,), (0,)), ((), ()))
contract_cols = (((1,), (1,)), ((), ()))
everywhere = ("o", "c", "a", "r")


def dot_f32(left, right, dims=(((1,), (0,)), ((), ()))):
    return lax.dot_general(left, right, dims, preferred_element_type=jnp.float32)


def norm_parts(values):
    center = values - jnp.mean(values, axis=-1, keepdims=True)
    rate = lax.rsqrt(jnp.mean(center * center, axis=-1, keepdims=True) + norm_eps)
    return center * rate, rate


def norm_back(normed, rate, gain, grad):
    scaled = gain * grad
    average = jnp.mean(scaled, axis=-1, keepdims=True)
    along = jnp.mean(scaled * normed, axis=-1, keepdims=True)
    return rate * (scaled - average - normed * along)


def head_part(rows, head):
    lane = lax.broadcasted_iota(jnp.int32, rows.shape, 1)
    return jnp.where(lane // HEAD_DIM == head, rows, jnp.zeros_like(rows))


def forward_kernel(low_ref, high_ref, q_ref, k_ref, v_ref, idq_ref, idk_ref, out_ref, lse_ref):
    block = pl.program_id(1)
    queries = q_ref[...]
    heads = queries.shape[1] // HEAD_DIM
    rows = queries.shape[0]
    parts = [head_part(queries, head) for head in range(heads)]
    ids_query = idq_ref[...]

    def step(index, carry):
        start = pl.multiple_of(index * key_rows, key_rows)
        keys = k_ref[pl.ds(start, key_rows), :]
        values = v_ref[pl.ds(start, key_rows), :].T
        same = idk_ref[pl.ds(start, key_rows), :] == ids_query
        result = []
        for head in range(heads):
            top, total, acc = carry[head]
            scores = jnp.where(same, dot_f32(keys, parts[head], contract_cols), mask_fill)
            new_top = jnp.maximum(top, jnp.max(scores, axis=0, keepdims=True))
            expon = jnp.exp(scores - new_top)
            shrink = jnp.exp(top - new_top)
            total = shrink * total + jnp.sum(expon, axis=0, keepdims=True)
            mine = values[head * HEAD_DIM : (head + 1) * HEAD_DIM]
            acc = shrink * acc + dot_f32(mine, expon.astype(jnp.bfloat16))
            result.append((new_top, total, acc))
        return tuple(result)

    start_carry = tuple(
        (
            jnp.full((1, rows), mask_fill, jnp.float32),
            jnp.zeros((1, rows), jnp.float32),
            jnp.zeros((HEAD_DIM, rows), jnp.float32),
        )
        for _ in range(heads)
    )
    final = lax.fori_loop(low_ref[block], high_ref[block], step, start_carry)
    merged = jnp.concatenate([acc / total for _, total, acc in final], axis=0)
    out_ref[...] = merged.T.astype(out_ref.dtype)
    lse_ref[0, 0] = jnp.concatenate([top + jnp.log(total) for top, total, _ in final], axis=0)


def backward_kernel(
    low_ref, high_ref, q_ref, k_ref, v_ref, idq_ref, idk_ref, att_ref, d_att_ref, lse_ref,
    dq_ref, dk_ref, dv_ref, dk_sum, dv_sum,
):
    block = pl.program_id(1)

    @pl.when(block == 0)
    def _():
        dk_sum[...] = jnp.zeros_like(dk_sum)
        dv_sum[...] = jnp.zeros_like(dv_sum)

    queries, d_att = q_ref[...], d_att_ref[...]
    heads = queries.shape[1] // HEAD_DIM
    rows = queries.shape[0]
    parts = [head_part(queries, head) for head in range(heads)]
    d_parts = [head_part(d_att, head) for head in range(heads)]
    ids_query = idq_ref[...]
    products = (att_ref[...].astype(jnp.float32) * d_att.astype(jnp.float32)).T
    inner = [
        jnp.sum(products[head * HEAD_DIM : (head + 1) * HEAD_DIM], axis=0, keepdims=True)
        for head in range(heads)
    ]
    lse = lse_ref[0, 0]

    def step(index, carry):
        start = pl.multiple_of(index * key_rows, key_rows)
        here = pl.ds(start, key_rows)
        keys, values = k_ref[here, :], v_ref[here, :]
        keys_turned = keys.T
        same = idk_ref[here, :] == ids_query
        result = []
        d_value, d_key = dv_sum[here, :], dk_sum[here, :]
        for head in range(heads):
            scores = jnp.where(same, dot_f32(keys, parts[head], contract_cols), mask_fill)
            probs = jnp.exp(scores - lse[head : head + 1])
            d_probs = dot_f32(values, d_parts[head], contract_cols)
            d_scores = (probs * (d_probs - inner[head])).astype(jnp.bfloat16)
            d_value = d_value + dot_f32(probs.astype(jnp.bfloat16), d_parts[head])
            d_key = d_key + dot_f32(d_scores, parts[head])
            mine = keys_turned[head * HEAD_DIM : (head + 1) * HEAD_DIM]
            result.append(carry[head] + dot_f32(mine, d_scores))
        dv_sum[here, :] = d_value
        dk_sum[here, :] = d_key
        return tuple(result)

    empty = tuple(jnp.zeros((HEAD_DIM, rows), jnp.float32) for _ in range(heads))
    final = lax.fori_loop(low_ref[block], high_ref[block], step, empty)
    dq_ref[...] = (jnp.concatenate(final, axis=0).T * 0.125).astype(dq_ref.dtype)

    @pl.when(block == pl.num_programs(1) - 1)
    def _():
        dk_ref[...] = dk_sum[...].astype(dk_ref.dtype)
        dv_ref[...] = dv_sum[...].astype(dv_ref.dtype)


def column_specs(tok_count, col_blocks, group=0):
    q_spec = pl.BlockSpec((query_rows, 128), lambda g, i, *_: (i, group + g))
    k_spec = pl.BlockSpec((tok_count, 128), lambda g, i, *_: (0, col_blocks + group + g))
    v_spec = pl.BlockSpec((tok_count, 128), lambda g, i, *_: (0, 2 * col_blocks + group + g))
    idq_spec = pl.BlockSpec((1, query_rows), lambda g, i, *_: (0, i))
    idk_spec = pl.BlockSpec((tok_count, 1), lambda g, i, *_: (0, 0))
    lse_spec = pl.BlockSpec(
        (1, 1, 128 // HEAD_DIM, query_rows), lambda g, i, *_: (group + g, i, 0, 0)
    )
    return q_spec, k_spec, v_spec, idq_spec, idk_spec, lse_spec


def attention(qkv, bounds, ids_row, ids_col):
    tok_count, cols3 = qkv.shape
    cols = cols3 // 3
    blocks, groups = tok_count // query_rows, cols // 128
    q_spec, k_spec, v_spec, idq_spec, idk_spec, lse_spec = column_specs(tok_count, groups)
    pairs = tok_count * tok_count // 2
    return pl.pallas_call(
        forward_kernel,
        grid_spec=pltpu.PrefetchScalarGridSpec(
            num_scalar_prefetch=2,
            grid=(groups, blocks),
            in_specs=[q_spec, k_spec, v_spec, idq_spec, idk_spec],
            out_specs=[q_spec, lse_spec],
        ),
        out_shape=[
            jax.ShapeDtypeStruct((tok_count, cols), jnp.bfloat16),
            jax.ShapeDtypeStruct((groups, blocks, 128 // HEAD_DIM, query_rows), jnp.float32),
        ],
        compiler_params=pltpu.CompilerParams(vmem_limit_bytes=40 * 1024 * 1024),
        cost_estimate=pl.CostEstimate(
            flops=pairs * 32 * cols, bytes_accessed=2 * qkv.size, transcendentals=2 * pairs
        ),
    )(*bounds, qkv, qkv, qkv, ids_row, ids_col)


def attention_back(qkv, bounds, ids_row, ids_col, att, d_att, lse, group):
    tok_count, cols3 = qkv.shape
    cols = cols3 // 3
    blocks, groups = tok_count // query_rows, cols // 128
    q_spec, k_spec, v_spec, idq_spec, idk_spec, lse_spec = column_specs(tok_count, groups, group)
    pairs = tok_count * tok_count // 2
    out_spec = pl.BlockSpec((query_rows, 128), lambda g, i, *_: (i, 0))
    out_whole = pl.BlockSpec((tok_count, 128), lambda g, i, *_: (0, 0))
    one = jax.ShapeDtypeStruct((tok_count, 128), jnp.bfloat16)
    return pl.pallas_call(
        backward_kernel,
        grid_spec=pltpu.PrefetchScalarGridSpec(
            num_scalar_prefetch=2,
            grid=(1, blocks),
            in_specs=[q_spec, k_spec, v_spec, idq_spec, idk_spec, q_spec, q_spec, lse_spec],
            out_specs=[out_spec, out_whole, out_whole],
            scratch_shapes=[
                pltpu.VMEM((tok_count, 128), jnp.float32),
                pltpu.VMEM((tok_count, 128), jnp.float32),
            ],
        ),
        out_shape=[one, one, one],
        compiler_params=pltpu.CompilerParams(vmem_limit_bytes=48 * 1024 * 1024),
        cost_estimate=pl.CostEstimate(
            flops=pairs * 40 * 128, bytes_accessed=4 * qkv.size, transcendentals=2 * pairs
        ),
    )(*bounds, qkv, qkv, qkv, ids_row, ids_col, att, d_att, lse)


pieces = 2


def entry_kernel(
    outer_count, rest_count, tok_ref, w_in_ref, pack_ref, ids_ref, x_ref, w_ref, packs_ref, ids_out_ref,
    ids_send, ids_recv, ids_sem,
    pack_sem, pack_send, pack_recv, packs_send, packs_recv, move_send, move_recv, rest_send, rest_recv, core_send, core_recv,
    w_send, w_recv, outer_send, outer_recv, own_sem,
):
    o, c, a, r = (lax.axis_index(name) for name in everywhere)
    rows = tok_ref.shape[1]
    part = rows // pieces
    w_rows = w_in_ref.shape[1]
    half, low = a // 2, a % 2
    counts = (outer_count, 2, 4, rest_count)
    here_spot = (o, c, a, r)
    dp_shifts = [(i, j, 0, 0) for i in range(outer_count) for j in range(2)][1:]
    tensor_shifts = [(0, 0, i, j) for i in range(4) for j in range(rest_count)][1:]
    core_shifts = [(0, i, j, 0) for i in range(2) for j in range(4)][1:]

    def away(shift):
        return tuple((spot + s) % n for spot, s, n in zip(here_spot, shift, counts))

    def back(shift):
        return tuple((spot - s + n) % n for spot, s, n in zip(here_spot, shift, counts))

    partners = [away(shift) for shift in sorted({*dp_shifts, *tensor_shifts, *core_shifts})]
    barrier = pltpu.get_barrier_semaphore()
    for partner in partners:
        pl.semaphore_signal(barrier, inc=1, device_id=partner, device_id_type=pl.DeviceIdType.MESH)
    pl.semaphore_wait(barrier, len(partners))
    peer = (o, 1 - c, a, r)

    def remote(src, dst, send, recv, target):
        return pltpu.make_async_remote_copy(
            src_ref=src, dst_ref=dst, send_sem=send, recv_sem=recv,
            device_id=target, device_id_type=pl.DeviceIdType.MESH,
        )

    def pack_spot(spot):
        return packs_ref.at[spot[2] * rest_count + spot[3], spot[0] * 2 + spot[1]]

    def pack_group(spot):
        return packs_ref.at[spot[2] * rest_count + spot[3]]

    def pack_copy(i):
        return remote(
            pack_ref, pack_spot(here_spot), pack_send.at[i], pack_recv.at[i], away(dp_shifts[i])
        )

    def packs_copy(i):
        mine = pack_group(here_spot)
        return remote(mine, mine, packs_send.at[i], packs_recv.at[i], away(tensor_shifts[i]))

    pack_own = pltpu.make_async_copy(pack_ref, pack_spot(here_spot), pack_sem)
    pack_own.start()
    ids_own = pltpu.make_async_copy(ids_ref, ids_out_ref.at[c], ids_sem)
    ids_own.start()
    ids_copy = remote(ids_ref, ids_out_ref.at[c], ids_send, ids_recv, peer)
    ids_copy.start()
    for i in range(len(dp_shifts)):
        pack_copy(i).start()

    def x_rows(seq_spot, rest_spot, piece):
        start = (seq_spot * rest_count + rest_spot) * rows + piece * part
        return x_ref.at[pl.ds(pl.multiple_of(start, part), part), :]

    def tok_rows(batch, piece):
        return tok_ref.at[batch, pl.ds(piece * part, part), :]

    def own_copy(batch, piece):
        return pltpu.make_async_copy(
            tok_rows(batch, piece), x_rows(a, r, piece), own_sem.at[piece]
        )

    def move_copy(batch, piece):
        return remote(
            tok_rows(batch, piece), x_rows(a, r, piece),
            move_send.at[batch, piece], move_recv.at[low, piece], (o, half, 2 * batch + c, r),
        )

    def stays(batch):
        return jnp.logical_and(half == c, 2 * batch + c == a)

    for piece in range(pieces):
        for batch in range(2):
            @pl.when(stays(batch))
            def _():
                own_copy(batch, piece).start()

            @pl.when(jnp.logical_not(stays(batch)))
            def _():
                move_copy(batch, piece).start()

    def w_spot(outer_spot, core_spot, turn):
        start = pl.multiple_of((outer_spot * 2 + core_spot) * w_rows, w_rows)
        return w_ref.at[turn, :, pl.ds(start, w_rows), :]

    w_own = pltpu.make_async_copy(w_in_ref, w_spot(o, c, low), own_sem.at[pieces])

    def w_copy(target):
        return remote(
            w_in_ref, w_spot(o, c, low), w_send.at[target], w_recv.at[c, low], (o, half, target, r)
        )

    for target in range(4):
        same = jnp.logical_and(half == c, a == target)

        @pl.when(same)
        def _():
            w_own.start()

        @pl.when(jnp.logical_not(same))
        def _():
            w_copy(target).start()

    pack_own.wait()
    for i, shift in enumerate(dp_shifts):
        spot = pack_spot(back(shift))
        remote(spot, spot, pack_send.at[i], pack_recv.at[i], peer).wait_recv()
    for i in range(len(tensor_shifts)):
        packs_copy(i).start()

    def rest_copy(turn, piece, shift):
        here = x_rows(2 * c + turn, r, piece)
        return remote(
            here, here, rest_send.at[turn, piece, shift - 1], rest_recv.at[turn, piece, shift - 1],
            (o, c, a, (r + shift) % rest_count),
        )

    def rest_landed(turn, piece, shift):
        here = x_rows(2 * c + turn, (r - shift + rest_count) % rest_count, piece)
        return remote(
            here, here, rest_send.at[turn, piece, shift - 1], rest_recv.at[turn, piece, shift - 1],
            peer,
        )

    def core_copy(turn, piece, shift, core):
        here = x_rows(2 * core + turn, (r - shift + rest_count) % rest_count, piece)
        return remote(
            here, here, core_send.at[turn, piece, shift], core_recv.at[turn, piece, shift], peer
        )

    for piece in range(pieces):
        for turn in range(2):
            same = jnp.logical_and(low == c, 2 * c + turn == a)

            @pl.when(same)
            def _():
                own_copy(0, piece).wait()

            @pl.when(jnp.logical_not(same))
            def _():
                here = x_rows(2 * c + turn, r, piece)
                remote(
                    here, here, move_send.at[0, piece], move_recv.at[turn, piece], peer
                ).wait_recv()

            for shift in range(1, rest_count):
                rest_copy(turn, piece, shift).start()
            core_copy(turn, piece, 0, c).start()

    def outer_copy(core, shift, outer_spot):
        start = pl.multiple_of((outer_spot * 2 + core) * w_rows, w_rows)
        here = w_ref.at[:, :, pl.ds(start, w_rows), :]
        return remote(
            here, here, outer_send.at[core, shift - 1], outer_recv.at[core, shift - 1],
            ((o + shift) % outer_count, c, a, r),
        )

    for core in range(2):
        for turn in range(2):
            same = jnp.logical_and(
                half == c, jnp.logical_and(c == core, low == turn)
            )

            @pl.when(same)
            def _():
                w_own.wait()

            @pl.when(jnp.logical_not(same))
            def _():
                here = w_spot(o, core, turn)
                remote(here, here, w_send.at[0], w_recv.at[core, turn], peer).wait_recv()
        for shift in range(1, outer_count):
            outer_copy(core, shift, o).start()

    for piece in range(pieces):
        for turn in range(2):
            for shift in range(1, rest_count):
                rest_landed(turn, piece, shift).wait_recv()
                core_copy(turn, piece, shift, c).start()

    for core in range(2):
        for shift in range(1, outer_count):
            outer_copy(core, shift, (o - shift + outer_count) % outer_count).wait_recv()
    for piece in range(pieces):
        for turn in range(2):
            for shift in range(rest_count):
                core_copy(turn, piece, shift, 1 - c).wait_recv()

    for piece in range(pieces):
        for batch in range(2):
            @pl.when(jnp.logical_not(stays(batch)))
            def _():
                move_copy(batch, piece).wait_send()
        for turn in range(2):
            for shift in range(1, rest_count):
                rest_copy(turn, piece, shift).wait_send()
            for shift in range(rest_count):
                core_copy(turn, piece, shift, c).wait_send()
    for target in range(4):
        @pl.when(jnp.logical_not(jnp.logical_and(half == c, a == target)))
        def _():
            w_copy(target).wait_send()
    for core in range(2):
        for shift in range(1, outer_count):
            outer_copy(core, shift, o).wait_send()
    for i in range(len(dp_shifts)):
        pack_copy(i).wait_send()
    ids_own.wait()
    ids_copy.wait_send()
    remote(ids_ref, ids_out_ref.at[1 - c], ids_send, ids_recv, peer).wait_recv()
    for i, shift in enumerate(tensor_shifts):
        spot = pack_group(back(shift))
        remote(spot, spot, packs_send.at[i], packs_recv.at[i], peer).wait_recv()
        packs_copy(i).wait_send()


def entry(tokens, qkv_weight, pack, ids):
    outer_count, rest_count = lax.axis_size("o"), lax.axis_size("r")
    batches, rows, width = tokens.shape
    dma = pltpu.SemaphoreType.DMA
    wide, narrow = max(rest_count - 1, 1), max(outer_count - 1, 1)
    return pl.pallas_call(
        lambda *refs: entry_kernel(outer_count, rest_count, *refs),
        in_specs=[pl.BlockSpec(memory_space=pl.ANY)] * 4,
        out_specs=[pl.BlockSpec(memory_space=pl.ANY)] * 4,
        out_shape=[
            jax.ShapeDtypeStruct((4 * rest_count * rows, width), tokens.dtype),
            jax.ShapeDtypeStruct(
                (2, qkv_weight.shape[0], width, qkv_weight.shape[2]), qkv_weight.dtype
            ),
            jax.ShapeDtypeStruct((4 * rest_count, 2 * outer_count, *pack.shape), pack.dtype),
            jax.ShapeDtypeStruct((2, *ids.shape), ids.dtype),
        ],
        scratch_shapes=[
            dma(()), dma(()), dma(()),
            dma(()), dma((2 * outer_count - 1,)), dma((2 * outer_count - 1,)),
            dma((4 * rest_count - 1,)), dma((4 * rest_count - 1,)),
            dma((2, pieces)), dma((2, pieces)),
            dma((2, pieces, wide)), dma((2, pieces, wide)),
            dma((2, pieces, rest_count)), dma((2, pieces, rest_count)),
            dma((4,)), dma((2, 2)), dma((2, narrow)), dma((2, narrow)), dma((pieces + 1,)),
        ],
        compiler_params=pltpu.CompilerParams(collective_id=0, has_side_effects=True),
        cost_estimate=pl.CostEstimate(
            flops=0, bytes_accessed=200 * 1024 * 1024, transcendentals=0
        ),
    )(tokens, qkv_weight, pack, ids)


def tail_kernel(
    outer_count, rest_count, groups, sums_ref, gain_ref, x_ref, d_mid_ref, w_ref, h_ref, mlp_ref,
    proj_ref, *refs,
):
    d_refs, refs = refs[: 3 * groups], refs[3 * groups :]
    total_ref, out_ref, shard_ref, fc1_ref, fc2_ref, proj_out_ref = refs[:6]
    (
        core_buf, core_got, rest_buf, rest_got, own_sum, grad_buf, grad_got, seq_buf, seq_got,
        moved, lines, dp_got, part, tensor_got, proj_got,
        core_send, core_recv, rest_send, rest_recv, grad_send, grad_recv, seq_send, seq_recv,
        seq_own, dp_send, dp_recv, tensor_send, tensor_recv, move_send, move_recv, own_sem,
        proj_send, proj_recv,
    ) = refs[6:]
    o, c, a, r = (lax.axis_index(name) for name in everywhere)
    half, low = a // 2, a % 2
    counts = (outer_count, 2, 4, rest_count)
    here_spot = (o, c, a, r)
    dp_shifts = [(i, j, 0, 0) for i in range(outer_count) for j in range(2)][1:]
    tensor_shifts = [(0, 0, i, j) for i in range(4) for j in range(rest_count)][1:]
    core_shifts = [(0, i, j, 0) for i in range(2) for j in range(4)][1:]

    def away(shift):
        return tuple((spot + s) % n for spot, s, n in zip(here_spot, shift, counts))

    partners = [away(shift) for shift in sorted({*dp_shifts, *tensor_shifts, *core_shifts})]
    barrier = pltpu.get_barrier_semaphore()
    for partner in partners:
        pl.semaphore_signal(barrier, inc=1, device_id=partner, device_id_type=pl.DeviceIdType.MESH)
    pl.semaphore_wait(barrier, len(partners))
    peer = (o, 1 - c, a, r)
    rows = x_ref.shape[1]
    own_cols = 128 * groups
    cols = own_cols // 2
    dp_count = 2 * outer_count
    shard_rows = w_ref.shape[0] // dp_count

    def remote(src, dst, send, recv, target):
        return pltpu.make_async_remote_copy(
            src_ref=src, dst_ref=dst, send_sem=send, recv_sem=recv,
            device_id=target, device_id_type=pl.DeviceIdType.MESH,
        )

    def d_rows(i, spot):
        return jnp.concatenate([d_refs[3 * g + i][spot, :] for g in range(groups)], axis=1)

    def partial(core, turn, shift):
        start = ((2 * core + turn) * rest_count + (r + shift) % rest_count) * rows
        spot = pl.ds(pl.multiple_of(start, rows), rows)
        total = 0.0
        for i in range(3):
            weight = w_ref[:, i * own_cols : (i + 1) * own_cols]
            total = total + dot_f32(d_rows(i, spot), weight, contract_cols)
        return total

    def core_copy(slot):
        return remote(
            core_buf.at[slot], core_got.at[slot], core_send.at[slot], core_recv.at[slot], peer
        )

    def rest_copy(turn, shift):
        return remote(
            rest_buf.at[shift - 1, turn], rest_got.at[shift - 1, turn],
            rest_send.at[shift - 1, turn], rest_recv.at[shift - 1, turn],
            (o, c, a, (r + shift) % rest_count),
        )

    def proj_copy(shift):
        target = (a + shift) % 4
        return remote(
            proj_ref.at[target], proj_got.at[shift - 1], proj_send.at[shift - 1],
            proj_recv.at[shift - 1], (o, c, target, r),
        )

    order = [*range(1, rest_count), 0]
    for shift in order:
        for turn in range(2):
            slot = 2 * shift + turn
            core_buf[slot] = partial(1 - c, turn, shift).astype(jnp.bfloat16)
            core_copy(slot).start()
    for shift in order:
        for turn in range(2):
            slot = 2 * shift + turn
            mine = partial(c, turn, shift)
            core_copy(slot).wait_recv()
            mine = mine + core_got[slot].astype(jnp.float32)
            if shift:
                rest_buf[shift - 1, turn] = mine.astype(jnp.bfloat16)
                rest_copy(turn, shift).start()
            else:
                own_sum[turn] = mine

    for shift in range(1, 4):
        proj_copy(shift).start()

    def grad_copy(shift):
        target = (o + shift) % outer_count
        return remote(
            grad_buf.at[target], grad_got.at[shift - 1], grad_send.at[shift - 1],
            grad_recv.at[shift - 1], (target, c, a, r),
        )

    for d in range(dp_count):
        turned = h_ref[:, d * shard_rows : (d + 1) * shard_rows].T
        for i in range(3):
            grad = dot_f32(turned, d_rows(i, slice(None)))
            grad_buf[d // 2, d % 2, :, i * own_cols : (i + 1) * own_cols] = grad.astype(
                jnp.bfloat16
            )
    for shift in range(1, outer_count):
        grad_copy(shift).start()

    total = 0.0
    for seq in range(4):
        total = total + mlp_ref[seq, 0].astype(jnp.float32)
    fc1_ref[...] = total
    total = 0.0
    for seq in range(4):
        total = total + mlp_ref[seq, 1].astype(jnp.float32)
    fc2_ref[...] = total.T
    total = proj_ref[a].astype(jnp.float32)
    for shift in range(1, 4):
        proj_copy(shift).wait_recv()
        total = total + proj_got[shift - 1].astype(jnp.float32)
    proj_out_ref[...] = total.T

    def stays(turn):
        return jnp.logical_and(low == c, 2 * c + turn == a)

    def move_copy(turn):
        return remote(
            moved.at[turn], out_ref.at[half], move_send.at[turn], move_recv.at[half],
            (o, low, 2 * c + turn, r),
        )

    stay_copy = pltpu.make_async_copy(moved.at[low], out_ref.at[half], own_sem)

    def settle_rows(turn):
        total = own_sum[turn]
        for shift in range(1, rest_count):
            rest_copy(turn, shift).wait_recv()
            total = total + rest_got[shift - 1, turn].astype(jnp.float32)
        normed, rate = norm_parts(x_ref[turn].astype(jnp.float32))
        grad = d_mid_ref[turn] + norm_back(normed, rate, gain_ref[...], total)
        moved[turn] = grad.astype(jnp.bfloat16)

        @pl.when(stays(turn))
        def _():
            stay_copy.start()

        @pl.when(jnp.logical_not(stays(turn)))
        def _():
            move_copy(turn).start()

        gain = jnp.sum(total * normed, axis=0, keepdims=True)
        return gain, jnp.sum(total, axis=0, keepdims=True)

    def mine(block):
        return jnp.logical_and(block // 2 == c, 2 * c + block % 2 == a)

    def seq_copy(block):
        return remote(
            seq_buf.at[block], seq_got.at[a], seq_send.at[block], seq_recv.at[a],
            (o, block // 2, 2 * c + block % 2, r),
        )

    def seq_keep(block):
        return pltpu.make_async_copy(seq_buf.at[block], seq_got.at[a], seq_own)

    first = settle_rows(0)
    for shift in range(1, outer_count):
        grad_copy(shift).wait_recv()
    for core in range(2):
        total = grad_buf[o, core].astype(jnp.float32)
        for shift in range(1, outer_count):
            total = total + grad_got[shift - 1, core].astype(jnp.float32)
        for turn in range(2):
            block = 2 * core + turn
            for i in range(3):
                start = i * own_cols + turn * cols
                seq_buf[block, i] = total[:, start : start + cols].astype(jnp.bfloat16)

            @pl.when(mine(block))
            def _():
                seq_keep(block).start()

            @pl.when(jnp.logical_not(mine(block)))
            def _():
                seq_copy(block).start()
    second = settle_rows(1)

    lines[...] = sums_ref[...]
    for i in range(2):
        line = first[i] + second[i]
        for d in range(dp_count):
            lines[d, i : i + 1, :] = line[:, d * shard_rows : (d + 1) * shard_rows]

    def dp_copy(i):
        target = away(dp_shifts[i])
        return remote(
            lines.at[target[0] * 2 + target[1]], dp_got.at[i], dp_send.at[i], dp_recv.at[i],
            target,
        )

    for i in range(len(dp_shifts)):
        dp_copy(i).start()
    total = lines[o * 2 + c]
    for i in range(len(dp_shifts)):
        dp_copy(i).wait_recv()
        total = total + dp_got[i]
    part[...] = total

    def tensor_copy(i):
        return remote(
            part, tensor_got.at[i], tensor_send.at[i], tensor_recv.at[i], away(tensor_shifts[i])
        )

    for i in range(len(tensor_shifts)):
        tensor_copy(i).start()
    for i in range(len(tensor_shifts)):
        tensor_copy(i).wait_recv()
        total = total + tensor_got[i]
    total_ref[...] = total

    for block in range(4):
        @pl.when(mine(block))
        def _():
            seq_keep(block).wait()
    for seq in range(4):
        here = jnp.logical_and(half == c, a == seq)

        @pl.when(jnp.logical_not(here))
        def _():
            spot = seq_got.at[seq]
            remote(spot, spot, seq_send.at[0], seq_recv.at[seq], peer).wait_recv()
    total = 0.0
    for seq in range(4):
        total = total + seq_got[seq].astype(jnp.float32)
    shard_ref[...] = total

    for batch in range(2):
        same = jnp.logical_and(half == c, 2 * batch + c == a)

        @pl.when(same)
        def _():
            stay_copy.wait()

        @pl.when(jnp.logical_not(same))
        def _():
            spot = out_ref.at[batch]
            remote(spot, spot, move_send.at[0], move_recv.at[batch], peer).wait_recv()
    for turn in range(2):
        @pl.when(jnp.logical_not(stays(turn)))
        def _():
            move_copy(turn).wait_send()
    for block in range(4):
        @pl.when(jnp.logical_not(mine(block)))
        def _():
            seq_copy(block).wait_send()
    for shift in order:
        for turn in range(2):
            core_copy(2 * shift + turn).wait_send()
            if shift:
                rest_copy(turn, shift).wait_send()
    for shift in range(1, outer_count):
        grad_copy(shift).wait_send()
    for shift in range(1, 4):
        proj_copy(shift).wait_send()
    for i in range(len(dp_shifts)):
        dp_copy(i).wait_send()
    for i in range(len(tensor_shifts)):
        tensor_copy(i).wait_send()


def tail(sums, gain, x, d_mid, w_qkv, h, mlp_parts, proj_parts, d_parts):
    outer, rest = lax.axis_size("o"), lax.axis_size("r")
    dma = pltpu.SemaphoreType.DMA
    few, many = 2 * outer - 1, 4 * rest - 1
    wide, narrow = max(rest - 1, 1), max(outer - 1, 1)
    shape = sums.shape[1:]
    _, rows, width = x.shape
    groups = len(d_parts) // 3
    own_cols, shard_rows = 128 * groups, width // (2 * outer)
    low = jnp.bfloat16
    space = pl.BlockSpec(memory_space=pltpu.VMEM)
    return pl.pallas_call(
        lambda *refs: tail_kernel(outer, rest, groups, *refs),
        in_specs=[space] * (8 + 3 * groups),
        out_specs=[space, pl.BlockSpec(memory_space=pl.ANY)] + [space] * 4,
        out_shape=[
            jax.ShapeDtypeStruct(shape, jnp.float32),
            jax.ShapeDtypeStruct(x.shape, low),
            jax.ShapeDtypeStruct((3, shard_rows, own_cols // 2), jnp.float32),
            jax.ShapeDtypeStruct(mlp_parts.shape[2:], jnp.float32),
            jax.ShapeDtypeStruct(mlp_parts.shape[:1:-1], jnp.float32),
            jax.ShapeDtypeStruct(proj_parts.shape[:0:-1], jnp.float32),
        ],
        scratch_shapes=[
            pltpu.VMEM((2 * rest, rows, width), low), pltpu.VMEM((2 * rest, rows, width), low),
            pltpu.VMEM((wide, 2, rows, width), low), pltpu.VMEM((wide, 2, rows, width), low),
            pltpu.VMEM((2, rows, width), jnp.float32),
            pltpu.VMEM((outer, 2, shard_rows, 3 * own_cols), low),
            pltpu.VMEM((narrow, 2, shard_rows, 3 * own_cols), low),
            pltpu.VMEM((4, 3, shard_rows, own_cols // 2), low),
            pltpu.VMEM((4, 3, shard_rows, own_cols // 2), low),
            pltpu.VMEM((2, rows, width), low),
            pltpu.VMEM(sums.shape, jnp.float32),
            pltpu.VMEM((few, *shape), jnp.float32), pltpu.VMEM(shape, jnp.float32),
            pltpu.VMEM((many, *shape), jnp.float32),
            pltpu.VMEM((3, *proj_parts.shape[1:]), low),
            dma((2 * rest,)), dma((2 * rest,)), dma((wide, 2)), dma((wide, 2)),
            dma((narrow,)), dma((narrow,)), dma((4,)), dma((4,)), dma(()),
            dma((few,)), dma((few,)), dma((many,)), dma((many,)), dma((2,)), dma((2,)), dma(()),
            dma((3,)), dma((3,)),
        ],
        compiler_params=pltpu.CompilerParams(
            collective_id=1, has_side_effects=True, vmem_limit_bytes=56 * 1024 * 1024
        ),
        cost_estimate=pl.CostEstimate(
            flops=0, bytes_accessed=250 * 1024 * 1024, transcendentals=0
        ),
    )(sums, gain, x, d_mid, w_qkv, h, mlp_parts, proj_parts, *d_parts)


def mlp_kernel(
    outer_count, rest_count,
    h_ref, dm_ref, w1_ref, w2_ref, bias_ref, m_ref, dh_ref, kept1_ref, got1_ref, kept2_ref,
    got2_ref, dbias_ref, h_turned, dm_turned, kept, sent, got, send_sem, got_sem,
    own_sem, rest_send, rest_recv, outer_send, outer_recv,
):
    o, core, a, r = (lax.axis_index(name) for name in everywhere)
    block = pl.program_id(0)
    count = pl.num_programs(0) - 1
    slot, other = block % 2, (block + 1) % 2
    peer = (o, 1 - core, a, r)
    partners = [peer]
    partners += [(o, core, a, (r + i) % rest_count) for i in range(1, rest_count)]
    partners += [((o + i) % outer_count, core, a, r) for i in range(1, outer_count)]

    def to_rest(index):
        target = index % rest_count
        shift = (target - r + rest_count) % rest_count
        return pltpu.make_async_remote_copy(
            src_ref=got.at[index, 0], dst_ref=got1_ref.at[shift - 1, index // rest_count],
            send_sem=rest_send.at[index], recv_sem=rest_recv.at[shift - 1, index // rest_count],
            device_id=(o, core, a, target), device_id_type=pl.DeviceIdType.MESH,
        )

    def keep_rest(index):
        return pltpu.make_async_copy(
            got.at[index, 0], kept1_ref.at[index // rest_count], own_sem.at[0, index]
        )

    def to_outer(index, shift):
        target = (o + shift) % outer_count
        return pltpu.make_async_remote_copy(
            src_ref=got.at[index, 1, target], dst_ref=got2_ref.at[shift - 1, index],
            send_sem=outer_send.at[shift - 1, index], recv_sem=outer_recv.at[shift - 1, index],
            device_id=(target, core, a, r), device_id_type=pl.DeviceIdType.MESH,
        )

    def keep_outer(index):
        return pltpu.make_async_copy(
            got.at[index, 1, o], kept2_ref.at[index], own_sem.at[1, index]
        )

    def to_peer(index, turn):
        return pltpu.make_async_remote_copy(
            src_ref=sent.at[turn], dst_ref=got.at[index],
            send_sem=send_sem.at[turn], recv_sem=got_sem.at[index],
            device_id=peer, device_id_type=pl.DeviceIdType.MESH,
        )

    @pl.when(block == 0)
    def _():
        barrier = pltpu.get_barrier_semaphore()
        for partner in partners:
            pl.semaphore_signal(
                barrier, inc=1, device_id=partner, device_id_type=pl.DeviceIdType.MESH
            )
        pl.semaphore_wait(barrier, len(partners))
        h_turned[...] = h_ref[...].T
        dm_turned[...] = dm_ref[...].T
        m_ref[...] = jnp.zeros_like(m_ref)
        dh_ref[...] = jnp.zeros_like(dh_ref)

    @pl.when(block >= 2)
    def _():
        to_peer(block - 2, slot).wait_send()

    @pl.when(block < count)
    def _():
        dp_count, _, _, rows = w1_ref.shape
        pre, d_act = bias_ref[...], 0.0
        for d in range(dp_count):
            spot = slice(d * rows, (d + 1) * rows)
            pre = pre + dot_f32(h_ref[:, spot], w1_ref[d, 0], contract_cols)
        for d in range(dp_count):
            spot = slice(d * rows, (d + 1) * rows)
            d_act = d_act + dot_f32(dm_ref[:, spot], w2_ref[d, 0], contract_cols)
        spread = 0.5 * (1.0 + lax.erf(pre * 0.7071067811865476))
        act = (pre * spread).astype(jnp.bfloat16)
        slope = spread + pre * jnp.exp(-0.5 * pre * pre) * 0.3989422804014327
        d_pre = (d_act * slope).astype(jnp.bfloat16)
        dbias_ref[...] = jnp.sum(d_pre.astype(jnp.float32), axis=0, keepdims=True)
        for d in range(dp_count):
            spot = slice(d * rows, (d + 1) * rows)
            m_ref[:, spot] += dot_f32(act, w2_ref[d, 0])
            dh_ref[:, spot] += dot_f32(d_pre, w1_ref[d, 0])
        for d in range(dp_count):
            spot = slice(d * rows, (d + 1) * rows)
            grad1 = dot_f32(h_turned[spot, :], d_pre).astype(jnp.bfloat16)
            grad2 = dot_f32(dm_turned[spot, :], act).astype(jnp.bfloat16)

            @pl.when(core == d % 2)
            def _():
                kept[slot, 0, d // 2] = grad1
                kept[slot, 1, d // 2] = grad2

            @pl.when(core != d % 2)
            def _():
                sent[slot, 0, d // 2] = grad1
                sent[slot, 1, d // 2] = grad2

        to_peer(block, slot).start()

    @pl.when(block >= 1)
    def _():
        to_peer(block - 1, other).wait_recv()
        done = block - 1
        for turn in range(2):
            mine = kept[other, turn].astype(jnp.float32)
            both = mine + got[done, turn].astype(jnp.float32)
            got[done, turn] = both.astype(jnp.bfloat16)

        @pl.when(done % rest_count == r)
        def _():
            keep_rest(done).start()

        @pl.when(done % rest_count != r)
        def _():
            to_rest(done).start()

        keep_outer(done).start()
        for shift in range(1, outer_count):
            to_outer(done, shift).start()

    @pl.when(block == count)
    def _():
        to_peer(block - 1, other).wait_send()

        def settle(index, carry):
            @pl.when(index % rest_count == r)
            def _():
                keep_rest(index).wait()

            @pl.when(index % rest_count != r)
            def _():
                to_rest(index).wait_send()

            keep_outer(index).wait()
            for shift in range(1, outer_count):
                to_outer(index, shift).wait()
            return carry

        lax.fori_loop(0, 4 * rest_count, settle, 0)
        for seq in range(4):
            for shift in range(1, rest_count):
                spot = got1_ref.at[shift - 1, seq]
                pltpu.make_async_remote_copy(
                    src_ref=spot, dst_ref=spot, send_sem=rest_send.at[0],
                    recv_sem=rest_recv.at[shift - 1, seq],
                    device_id=peer, device_id_type=pl.DeviceIdType.MESH,
                ).wait_recv()


def mlp(rows_low, d_branch, weights, hid, bias):
    tokens_here, width = rows_low.shape
    dp_count, tensor_count, _, rows = weights.shape
    outer = dp_count // 2
    whole = pl.BlockSpec((tokens_here, width), lambda t: (0, 0))
    rest = tensor_count // 4
    far = pl.BlockSpec(memory_space=pl.ANY)
    wide, narrow = max(rest - 1, 1), max(outer - 1, 1)
    low = jnp.bfloat16
    dma = pltpu.SemaphoreType.DMA
    out = jax.ShapeDtypeStruct((tokens_here, width), jnp.float32)
    last = tensor_count - 1
    line = pl.BlockSpec((1, hid), lambda t: (0, jnp.minimum(t, last)))
    w1_spec = pl.BlockSpec((dp_count, 1, hid, rows), lambda t: (0, jnp.minimum(t, last), 0, 0))
    w2_spec = pl.BlockSpec((dp_count, 1, hid, rows), lambda t: (0, jnp.minimum(t, last), 1, 0))
    return pl.pallas_call(
        lambda *refs: mlp_kernel(outer, rest, *refs),
        grid=(tensor_count + 1,),
        in_specs=[whole, whole, w1_spec, w2_spec, line],
        out_specs=[whole, whole, far, far, far, far, line],
        out_shape=[
            out, out,
            jax.ShapeDtypeStruct((4, outer, rows, hid), low),
            jax.ShapeDtypeStruct((wide, 4, outer, rows, hid), low),
            jax.ShapeDtypeStruct((tensor_count, rows, hid), low),
            jax.ShapeDtypeStruct((narrow, tensor_count, rows, hid), low),
            jax.ShapeDtypeStruct((1, tensor_count * hid), jnp.float32),
        ],
        scratch_shapes=[
            pltpu.VMEM((width, tokens_here), jnp.bfloat16),
            pltpu.VMEM((width, tokens_here), jnp.bfloat16),
            pltpu.VMEM((2, 2, outer, rows, hid), jnp.bfloat16),
            pltpu.VMEM((2, 2, outer, rows, hid), jnp.bfloat16),
            pltpu.VMEM((tensor_count, 2, outer, rows, hid), jnp.bfloat16),
            dma((2,)), dma((tensor_count,)), dma((2, tensor_count)),
            dma((tensor_count,)), dma((wide, 4)),
            dma((narrow, tensor_count)), dma((narrow, tensor_count)),
        ],
        compiler_params=pltpu.CompilerParams(
            vmem_limit_bytes=60 * 1024 * 1024, collective_id=2, has_side_effects=True
        ),
        cost_estimate=pl.CostEstimate(
            flops=12 * tokens_here * width * tensor_count * hid,
            bytes_accessed=64 * 1024 * 1024,
            transcendentals=2 * tokens_here * tensor_count * hid,
        ),
    )(rows_low, d_branch, weights, weights, bias)


def proj_groups(weights_ref, rest_count):
    for group in range(weights_ref.shape[1] // 2):
        first = 2 * (group // rest_count) * rest_count + group % rest_count
        yield group, first, first + rest_count


def before_kernel(
    rest_count, att_ref, x_ref, dy_ref, weights_ref, vec_ref, mid_ref, branch_ref, h_ref, dm_ref
):
    dp_count, _, depth, rows = weights_ref.shape
    branch = []
    for d in range(dp_count):
        total = vec_ref[2:3, d * rows : (d + 1) * rows]
        for group, one, two in proj_groups(weights_ref, rest_count):
            weight = jnp.concatenate([weights_ref[d, one], weights_ref[d, two]], axis=0)
            total = total + dot_f32(att_ref[group], weight)
        branch.append(total)
    branch = jnp.concatenate(branch, axis=1)
    branch_ref[...] = branch
    middle = x_ref[...].astype(jnp.float32) + vec_ref[3:4] * branch
    mid_ref[...] = middle
    normed, _ = norm_parts(middle)
    h_ref[...] = (normed * vec_ref[4:5] + vec_ref[5:6]).astype(jnp.bfloat16)
    dm_ref[...] = (vec_ref[7:8] * dy_ref[...].astype(jnp.float32)).astype(jnp.bfloat16)


def after_kernel(
    rest_count, m_ref, dh_ref, mid_ref, branch_ref, dy_ref, att_ref, weights_ref, vec_ref,
    out_ref, d_mid_ref, d_att_ref, sums_ref, kept_ref, sent_ref, grad,
):
    step, core = pl.program_id(0), lax.axis_index("c")
    dp_count, _, depth, rows = weights_ref.shape

    @pl.when(step == 0)
    def _():
        sums_ref[...] = jnp.zeros_like(sums_ref)
        grad[...] = jnp.zeros_like(grad)

    middle, dy = mid_ref[...], dy_ref[...].astype(jnp.float32)
    two = m_ref[...] + vec_ref[6:7]
    out_ref[...] = (middle + vec_ref[7:8] * two).astype(jnp.bfloat16)
    dm = (vec_ref[7:8] * dy).astype(jnp.bfloat16).astype(jnp.float32)
    normed, rate = norm_parts(middle)
    d_normed = dh_ref[...]
    d_mid = dy + norm_back(normed, rate, vec_ref[4:5], d_normed)
    d_mid_ref[...] = d_mid
    d_branch = (vec_ref[3:4] * d_mid).astype(jnp.bfloat16)
    lines = [
        d_branch.astype(jnp.float32), d_mid * branch_ref[...], d_normed * normed, d_normed, dm,
        dy * two,
    ]
    for i, line in enumerate(lines):
        sums_ref[i : i + 1] += jnp.sum(line, axis=0, keepdims=True)
    turned = d_branch.T
    for group, one, two in proj_groups(weights_ref, rest_count):
        total = 0.0
        for d in range(dp_count):
            part = slice(d * rows, (d + 1) * rows)
            weight = jnp.concatenate([weights_ref[d, one], weights_ref[d, two]], axis=0)
            total = total + dot_f32(d_branch[:, part], weight, contract_cols)
        d_att_ref[group] = total.astype(jnp.bfloat16)
        both = dot_f32(turned, att_ref[group])
        grad[one] += both[:, :depth]
        grad[two] += both[:, depth:]

    @pl.when(step == pl.num_programs(0) - 1)
    def _():
        for d in range(dp_count):
            part = grad[:, d * rows : (d + 1) * rows].astype(jnp.bfloat16)

            @pl.when(core == d % 2)
            def _():
                kept_ref[:, d // 2] = part

            @pl.when(core != d % 2)
            def _():
                sent_ref[:, d // 2] = part


def side_specs(weights, own_cols, steps, own_rows, width):
    dp_count, tensor_count, total, rows = weights.shape
    depth = own_cols // 2
    tile = own_rows // steps
    groups = tensor_count // 2
    row_spec = pl.BlockSpec((tile, width), lambda i: (i, 0))
    att_spec = pl.BlockSpec((groups, tile, own_cols), lambda i: (0, i, 0))
    w_spec = pl.BlockSpec(
        (dp_count, tensor_count, depth, rows), lambda i: (0, 0, total // depth - 1, 0)
    )
    vec_spec = pl.BlockSpec((8, width), lambda i: (0, 0))
    return row_spec, att_spec, w_spec, vec_spec


side_steps = 2


def before(att, x, dy, weights, vecs):
    own_rows, width = x.shape
    rest = lax.axis_size("r")
    row_spec, att_spec, w_spec, vec_spec = side_specs(
        weights, att.shape[2], side_steps, own_rows, width
    )
    wide = jax.ShapeDtypeStruct((own_rows, width), jnp.float32)
    slim = jax.ShapeDtypeStruct((own_rows, width), jnp.bfloat16)
    return pl.pallas_call(
        lambda *refs: before_kernel(rest, *refs),
        grid=(side_steps,),
        in_specs=[att_spec, row_spec, row_spec, w_spec, vec_spec],
        out_specs=[row_spec] * 4,
        out_shape=[wide, wide, slim, slim],
        compiler_params=pltpu.CompilerParams(vmem_limit_bytes=48 * 1024 * 1024),
        cost_estimate=pl.CostEstimate(
            flops=4 * own_rows * width * width, bytes_accessed=16 * 1024 * 1024, transcendentals=0
        ),
    )(att, x, dy, weights, vecs)


def after(m, dh, middle, branch, dy, att, weights, vecs):
    own_rows, width = m.shape
    rest, outer = lax.axis_size("r"), lax.axis_size("o")
    tensor_count, rows = weights.shape[1], weights.shape[3]
    depth = att.shape[2] // 2
    row_spec, att_spec, w_spec, vec_spec = side_specs(
        weights, att.shape[2], side_steps, own_rows, width
    )
    grad_spec = pl.BlockSpec((tensor_count, outer, rows, depth), lambda i: (0, 0, 0, 0))
    grad = jax.ShapeDtypeStruct((tensor_count, outer, rows, depth), jnp.bfloat16)
    return pl.pallas_call(
        lambda *refs: after_kernel(rest, *refs),
        grid=(side_steps,),
        in_specs=[row_spec] * 5 + [att_spec, w_spec, vec_spec],
        out_specs=[row_spec, row_spec, att_spec, vec_spec, grad_spec, grad_spec],
        out_shape=[
            jax.ShapeDtypeStruct((own_rows, width), jnp.bfloat16),
            jax.ShapeDtypeStruct((own_rows, width), jnp.float32),
            jax.ShapeDtypeStruct(att.shape, jnp.bfloat16),
            jax.ShapeDtypeStruct((8, width), jnp.float32),
            grad, grad,
        ],
        scratch_shapes=[pltpu.VMEM((tensor_count, width, depth), jnp.float32)],
        compiler_params=pltpu.CompilerParams(vmem_limit_bytes=56 * 1024 * 1024),
        cost_estimate=pl.CostEstimate(
            flops=8 * own_rows * width * width, bytes_accessed=24 * 1024 * 1024, transcendentals=0
        ),
    )(m, dh, middle, branch, dy, att, weights, vecs)


def gather_parts(shard):
    parts = lax.all_gather(shard, everywhere, axis=0, tiled=False)
    return parts.reshape(lax.axis_size("o") * 2, -1, *shard.shape)


def pick(blocks, index):
    return lax.dynamic_index_in_dim(blocks, index, 0, keepdims=False)


def place_shift(step, count):
    return [(spot, (spot + step) % count) for spot in range(count)]


def move_pairs(step):
    pairs = []
    for core in range(2):
        for seq in range(4):
            batch = (seq % 2) ^ step
            pairs.append((core * 4 + seq, (seq // 2) * 4 + 2 * batch + core))
    return pairs


def move_in(both):
    low = lax.axis_index("a") % 2
    batch = lax.axis_index("a") // 2
    got = [
        lax.ppermute(pick(both, low ^ step), ("c", "a"), move_pairs(step)) for step in range(2)
    ]
    return jnp.stack([jnp.where(batch == 0, got[j], got[1 - j]) for j in range(2)])


def move_out(own):
    low = lax.axis_index("a") % 2
    batch = lax.axis_index("a") // 2
    got = [
        lax.ppermute(
            pick(own, batch ^ step), ("c", "a"), [(t, s) for s, t in move_pairs(step)]
        )
        for step in range(2)
    ]
    return jnp.stack([jnp.where(low == 0, got[b], got[1 - b]) for b in range(2)])


def sum_shards(blocks, axis, dim, dtype):
    count, me = blocks.shape[dim], lax.axis_index(axis)

    def block(spot):
        return lax.dynamic_index_in_dim(blocks, spot, dim, keepdims=False)

    got = [
        lax.ppermute(block((me + step) % count), axis, place_shift(step, count))
        for step in range(1, count)
    ]
    total = block(me).astype(jnp.float32)
    for values in got:
        total = total + values.astype(jnp.float32)
    return total.astype(dtype)


def seq_parts(blocks):
    me = lax.axis_index("a")
    parts = [pick(blocks, me)]
    for step in range(1, 4):
        parts.append(lax.ppermute(pick(blocks, (me + step) % 4), "a", place_shift(step, 4)))
    return parts


def pair_sum(kept, got, count):
    total = kept.astype(jnp.float32)
    for i in range(count):
        total = total + got[i].astype(jnp.float32)
    return total.astype(jnp.bfloat16)


def core_sum(own, sent):
    got = lax.ppermute(sent, "c", [(0, 1), (1, 0)])
    total = (own.astype(jnp.float32) + got.astype(jnp.float32)).astype(jnp.bfloat16)
    return total.reshape(4, lax.axis_size("r"), *total.shape[1:])


def body(
    tokens, segment_ids, out_grad, norm1_gain, norm1_bias, qkv_weight, qv_bias, proj_weight,
    proj_bias, scale1, norm2_gain, norm2_bias, fc1_weight, fc1_bias, fc2_weight, fc2_bias, scale2,
):
    o, c, a, r = (lax.axis_index(name) for name in everywhere)
    outer, rest = lax.axis_size("o"), lax.axis_size("r")
    dp_count, tensor_count = outer * 2, 4 * rest
    batches, rows_here, width = tokens.shape
    own_rows = 2 * rows_here
    tok_count = rows_here * tensor_count
    cols_here, shard_rows = qkv_weight.shape[2], qkv_weight.shape[1]
    own_cols = 2 * cols_here
    hidden = fc1_weight.shape[1] * tensor_count
    short, fc1_short = qv_bias.shape[1], fc1_bias.shape[0]

    vectors = jnp.stack(
        [norm1_gain, norm1_bias, proj_bias, scale1, norm2_gain, norm2_bias, fc2_bias, scale2]
    )
    small = jnp.concatenate([qv_bias.reshape(-1), fc1_bias])
    small = jnp.pad(small[None], ((0, 7), (0, shard_rows - small.shape[0])))
    seq_rows, w_parts, packs, ids = entry(
        tokens, qkv_weight, jnp.concatenate([vectors, small]), segment_ids
    )
    seq_rows, out_grad = lax.optimization_barrier((seq_rows, out_grad))
    vecs = jnp.moveaxis(packs[0, :, :8], 0, 1).reshape(8, width).astype(jnp.float32)
    biases = packs[:, :, 8].astype(jnp.float32)
    bias_fc1 = biases[:, :, 2 * short : 2 * short + fc1_short].reshape(hidden)
    bias_qv = biases[:, :, : 2 * short].reshape(2, 2, rest, dp_count, 2, short)
    bias_qv = lax.dynamic_index_in_dim(bias_qv, c, 0, keepdims=False)
    bias_qv = lax.dynamic_index_in_dim(bias_qv, r, 1, keepdims=False)
    bias_qv = jnp.moveaxis(bias_qv, 2, 0).reshape(2, own_cols)
    bias_qkv = jnp.concatenate([bias_qv[0], jnp.zeros_like(bias_qv[0]), bias_qv[1]])
    scale_qkv = jnp.concatenate([jnp.full((own_cols,), 0.125), jnp.ones((2 * own_cols,))])

    run_ids = pick(pick(ids, a % 2), a // 2)[0]
    blocks = tok_count // query_rows
    first = run_ids.reshape(blocks, query_rows)[:, :1]
    last = run_ids.reshape(blocks, query_rows)[:, -1:]
    low = jnp.sum((run_ids[None] < first).astype(jnp.int32), axis=-1) // key_rows
    reach = jnp.sum((run_ids[None] <= last).astype(jnp.int32), axis=-1)
    bounds = (low, (reach + key_rows - 1) // key_rows)
    ids_row, ids_col = run_ids[None, :], run_ids[:, None]

    weights = gather_parts(jnp.concatenate([fc1_weight.T, fc2_weight, proj_weight]))
    w_qkv = jnp.moveaxis(w_parts, 0, 2).swapaxes(0, 1).reshape(width, 3 * own_cols)

    def own_of(values):
        split = values.reshape(2, 2, rest, rows_here, values.shape[1])
        split = lax.dynamic_index_in_dim(split, c, 0, keepdims=False)
        split = lax.dynamic_index_in_dim(split, r, 1, keepdims=False)
        return split.reshape(own_rows, values.shape[1])

    normed_all, _ = norm_parts(seq_rows.astype(jnp.float32))
    normed_all_low = (normed_all * vecs[0] + vecs[1]).astype(jnp.bfloat16)
    qkv = ((dot_f32(normed_all_low, w_qkv) + bias_qkv) * scale_qkv).astype(jnp.bfloat16)
    grad_moved = move_in(out_grad)
    att_heads, lse = attention(qkv, bounds, ids_row, ids_col)

    rows_own = own_of(seq_rows)
    grad_top = grad_moved.reshape(own_rows, width)
    sent = att_heads.reshape(2, 2, rest, rows_here, own_cols)
    sent = jnp.swapaxes(sent, 1, 2).reshape(2 * rest, own_rows, own_cols)
    attended = lax.all_to_all(sent, ("c", "r"), split_axis=0, concat_axis=0, tiled=True)
    middle, branch_one, mlp_in, d_branch2 = before(attended, rows_own, grad_top, weights, vecs)
    branch_two, d_normed_two, kept1, got1, kept2, got2, d_fc1_bias = mlp(
        mlp_in, d_branch2, weights, fc2_weight.shape[0], bias_fc1[None]
    )
    grad_fc1 = pair_sum(kept1, got1, rest - 1)
    grad_fc2 = pair_sum(kept2, got2, outer - 1).reshape(4, rest, *kept2.shape[1:])
    branch_two, grad_fc1, grad_fc2 = lax.optimization_barrier((branch_two, grad_fc1, grad_fc2))
    grad_fc1 = sum_shards(grad_fc1, "o", 1, jnp.bfloat16)
    grad_fc2 = sum_shards(grad_fc2, "r", 1, jnp.bfloat16)
    block_out, d_middle, sent, line_sums, proj_kept, proj_sent = after(
        branch_two, d_normed_two, middle, branch_one, grad_top, attended, weights, vecs
    )
    d_heads = lax.all_to_all(sent, ("c", "r"), split_axis=0, concat_axis=0, tiled=True)
    d_heads = jnp.swapaxes(d_heads.reshape(2, rest, 2, rows_here, own_cols), 1, 2)
    d_heads = d_heads.reshape(tok_count, own_cols)
    grad_proj = core_sum(proj_kept, proj_sent)
    d_heads, grad_fc1, grad_fc2, grad_proj, block_out = lax.optimization_barrier(
        (d_heads, grad_fc1, grad_fc2, grad_proj, block_out)
    )

    block_out = move_out(block_out.reshape(2, rows_here, width))
    mlp_parts = jnp.stack([grad_fc1, grad_fc2], axis=1)
    mlp_parts = lax.all_to_all(mlp_parts, "a", split_axis=0, concat_axis=0, tiled=True)
    grad_proj = sum_shards(grad_proj, "o", 2, jnp.bfloat16)
    groups = own_cols // 128
    d_parts = []
    for group in range(groups):
        d_parts.append(
            attention_back(qkv, bounds, ids_row, ids_col, att_heads, d_heads, lse, group)
        )
        if group == 0:
            d_parts, d_heads, grad_proj = lax.optimization_barrier((d_parts, d_heads, grad_proj))
            grad_proj = sum_shards(grad_proj, "r", 1, jnp.bfloat16)
    d_parts, grad_proj, block_out, mlp_parts = lax.optimization_barrier(
        (d_parts, grad_proj, block_out, mlp_parts)
    )
    d_bias_qv = jnp.stack(
        [
            jnp.concatenate([jnp.sum(part[i].astype(jnp.float32), axis=0) for part in d_parts])
            for i in (0, 2)
        ]
    ).reshape(2, 2, cols_here)
    spread_qv = jnp.zeros((2, 2, 2, rest, cols_here), jnp.float32)
    spread_qv = lax.dynamic_update_slice(
        spread_qv, d_bias_qv[:, None, :, None], (0, c, 0, r, 0)
    )
    lines = jnp.concatenate([line_sums[6:], line_sums[:6]]).reshape(8, dp_count, shard_rows)
    fc1_lines = d_fc1_bias.reshape(tensor_count, dp_count, fc1_short)
    fc1_lines = jnp.swapaxes(fc1_lines, 0, 1).reshape(dp_count, -1, shard_rows)
    qv_lines = spread_qv.reshape(2, tensor_count, dp_count, short)
    qv_lines = jnp.moveaxis(qv_lines, 2, 0).reshape(dp_count, -1, shard_rows)
    sums = jnp.concatenate([jnp.swapaxes(lines, 0, 1), fc1_lines, qv_lines], axis=1)
    sums = jnp.pad(sums, ((0, 0), (0, -sums.shape[1] % 8), (0, 0)))
    vec_sums, input_grad, shard_qkv, shard_fc1, shard_fc2, shard_proj = tail(
        sums, vecs[:1], rows_own.reshape(2, rows_here, width),
        d_middle.reshape(2, rows_here, width), w_qkv, normed_all_low, mlp_parts, grad_proj,
        [values for part in d_parts for values in part],
    )
    place = a * rest + r
    fc1_rows = fc1_lines.shape[1]
    grad_fc1_bias = vec_sums[8 : 8 + fc1_rows].reshape(tensor_count, fc1_short)
    grad_fc1_bias = pick(grad_fc1_bias, place)
    grad_qv_bias = vec_sums[8 + fc1_rows : 8 + fc1_rows + qv_lines.shape[1]]
    grad_qv_bias = lax.dynamic_index_in_dim(
        grad_qv_bias.reshape(2, tensor_count, short), place, 1, keepdims=False
    )
    return (
        block_out,
        input_grad,
        vec_sums[0],
        vec_sums[1],
        shard_qkv,
        grad_qv_bias,
        shard_proj,
        vec_sums[2],
        vec_sums[3],
        vec_sums[4],
        vec_sums[5],
        shard_fc1,
        grad_fc1_bias,
        shard_fc2,
        vec_sums[6],
        vec_sums[7],
    )


def solution(mesh):
    dp, tensor = ("o", "c"), ("a", "r")
    dp_count, tensor_count = mesh.devices.shape
    finer = Mesh(mesh.devices.reshape(dp_count // 2, 2, 4, tensor_count // 4), everywhere)
    rows = P(None, everywhere, None)
    vec = P(dp)
    in_specs = (
        rows, P(None, dp, None), rows, vec, vec, P(None, dp, tensor), P(None, tensor + dp),
        P(tensor, dp), vec, vec, vec, vec, P(dp, tensor), P(tensor + dp), P(tensor, dp), vec, vec,
    )
    out_specs = (
        rows, rows, vec, vec, P(None, dp, tensor), P(None, tensor + dp), P(tensor, dp), vec, vec,
        vec, vec, P(dp, tensor), P(tensor + dp), P(tensor, dp), vec, vec,
    )
    return jax.shard_map(body, mesh=finer, in_specs=in_specs, out_specs=out_specs, check_vma=False)
```

```python
import jax
import jax.numpy as jnp
from jax import lax
from jax.experimental import pallas as pl
from jax.experimental.pallas import tpu as pltpu
from jax.sharding import Mesh, PartitionSpec as P

HEAD_DIM = 64

norm_eps = 1e-06
mask_fill = -1e30
query_rows = 512
back_rows = 256
key_rows = 512
contract_rows = (((0,), (0,)), ((), ()))
contract_cols = (((1,), (1,)), ((), ()))
everywhere = ("o", "c", "a", "r")


def dot_f32(left, right, dims=(((1,), (0,)), ((), ()))):
    return lax.dot_general(left, right, dims, preferred_element_type=jnp.float32)


def norm_parts(values):
    center = values - jnp.mean(values, axis=-1, keepdims=True)
    rate = lax.rsqrt(jnp.mean(center * center, axis=-1, keepdims=True) + norm_eps)
    return center * rate, rate


def norm_back(normed, rate, gain, grad):
    scaled = gain * grad
    average = jnp.mean(scaled, axis=-1, keepdims=True)
    along = jnp.mean(scaled * normed, axis=-1, keepdims=True)
    return rate * (scaled - average - normed * along)


def head_part(rows, head):
    lane = lax.broadcasted_iota(jnp.int32, rows.shape, 1)
    return jnp.where(lane // HEAD_DIM == head, rows, jnp.zeros_like(rows))


def forward_kernel(low_ref, high_ref, q_ref, k_ref, v_ref, idq_ref, idk_ref, out_ref, lse_ref):
    block = pl.program_id(1)
    queries = q_ref[...]
    heads = queries.shape[1] // HEAD_DIM
    rows = queries.shape[0]
    parts = [head_part(queries, head) for head in range(heads)]
    ids_query = idq_ref[...]

    def step(index, carry):
        start = pl.multiple_of(index * key_rows, key_rows)
        keys = k_ref[pl.ds(start, key_rows), :]
        values = v_ref[pl.ds(start, key_rows), :].T
        same = idk_ref[pl.ds(start, key_rows), :] == ids_query
        result = []
        for head in range(heads):
            top, total, acc = carry[head]
            scores = jnp.where(same, dot_f32(keys, parts[head], contract_cols), mask_fill)
            new_top = jnp.maximum(top, jnp.max(scores, axis=0, keepdims=True))
            expon = jnp.exp(scores - new_top)
            shrink = jnp.exp(top - new_top)
            total = shrink * total + jnp.sum(expon, axis=0, keepdims=True)
            mine = values[head * HEAD_DIM : (head + 1) * HEAD_DIM]
            acc = shrink * acc + dot_f32(mine, expon.astype(jnp.bfloat16))
            result.append((new_top, total, acc))
        return tuple(result)

    start_carry = tuple(
        (
            jnp.full((1, rows), mask_fill, jnp.float32),
            jnp.zeros((1, rows), jnp.float32),
            jnp.zeros((HEAD_DIM, rows), jnp.float32),
        )
        for _ in range(heads)
    )
    final = lax.fori_loop(low_ref[block], high_ref[block], step, start_carry)
    merged = jnp.concatenate([acc / total for _, total, acc in final], axis=0)
    out_ref[...] = merged.T.astype(out_ref.dtype)
    lse_ref[0, 0] = jnp.concatenate([top + jnp.log(total) for top, total, _ in final], axis=0)


def backward_kernel(
    low_ref, high_ref, q_ref, k_ref, v_ref, idq_ref, idk_ref, att_ref, d_att_ref, lse_ref,
    dq_ref, dk_ref, dv_ref, dk_sum, dv_sum,
):
    block = pl.program_id(1)

    @pl.when(block == 0)
    def _():
        dk_sum[...] = jnp.zeros_like(dk_sum)
        dv_sum[...] = jnp.zeros_like(dv_sum)

    queries, d_att = q_ref[...], d_att_ref[...]
    heads = queries.shape[1] // HEAD_DIM
    rows = queries.shape[0]
    parts = [head_part(queries, head) for head in range(heads)]
    d_parts = [head_part(d_att, head) for head in range(heads)]
    ids_query = idq_ref[...]
    products = (att_ref[...].astype(jnp.float32) * d_att.astype(jnp.float32)).T
    inner = [
        jnp.sum(products[head * HEAD_DIM : (head + 1) * HEAD_DIM], axis=0, keepdims=True)
        for head in range(heads)
    ]
    lse = lse_ref[0, 0]

    def step(index, carry):
        start = pl.multiple_of(index * key_rows, key_rows)
        here = pl.ds(start, key_rows)
        keys, values = k_ref[here, :], v_ref[here, :]
        keys_turned = keys.T
        same = idk_ref[here, :] == ids_query
        result = []
        d_value, d_key = dv_sum[here, :], dk_sum[here, :]
        for head in range(heads):
            scores = jnp.where(same, dot_f32(keys, parts[head], contract_cols), mask_fill)
            probs = jnp.exp(scores - lse[head : head + 1])
            d_probs = dot_f32(values, d_parts[head], contract_cols)
            d_scores = (probs * (d_probs - inner[head])).astype(jnp.bfloat16)
            d_value = d_value + dot_f32(probs.astype(jnp.bfloat16), d_parts[head])
            d_key = d_key + dot_f32(d_scores, parts[head])
            mine = keys_turned[head * HEAD_DIM : (head + 1) * HEAD_DIM]
            result.append(carry[head] + dot_f32(mine, d_scores))
        dv_sum[here, :] = d_value
        dk_sum[here, :] = d_key
        return tuple(result)

    empty = tuple(jnp.zeros((HEAD_DIM, rows), jnp.float32) for _ in range(heads))
    final = lax.fori_loop(low_ref[block], high_ref[block], step, empty)
    dq_ref[...] = (jnp.concatenate(final, axis=0).T * 0.125).astype(dq_ref.dtype)

    @pl.when(block == pl.num_programs(1) - 1)
    def _():
        dk_ref[...] = dk_sum[...].astype(dk_ref.dtype)
        dv_ref[...] = dv_sum[...].astype(dv_ref.dtype)


def column_specs(tok_count, col_blocks, rows, group=0):
    q_spec = pl.BlockSpec((rows, 128), lambda g, i, *_: (i, group + g))
    k_spec = pl.BlockSpec((tok_count, 128), lambda g, i, *_: (0, col_blocks + group + g))
    v_spec = pl.BlockSpec((tok_count, 128), lambda g, i, *_: (0, 2 * col_blocks + group + g))
    idq_spec = pl.BlockSpec((1, rows), lambda g, i, *_: (0, i))
    idk_spec = pl.BlockSpec((tok_count, 1), lambda g, i, *_: (0, 0))
    lse_spec = pl.BlockSpec(
        (1, 1, 128 // HEAD_DIM, rows), lambda g, i, *_: (group + g, i, 0, 0)
    )
    return q_spec, k_spec, v_spec, idq_spec, idk_spec, lse_spec


def attention(qkv, bounds, ids_row, ids_col):
    tok_count, cols3 = qkv.shape
    cols = cols3 // 3
    blocks, groups = tok_count // query_rows, cols // 128
    q_spec, k_spec, v_spec, idq_spec, idk_spec, lse_spec = column_specs(tok_count, groups, query_rows)
    pairs = tok_count * tok_count // 2
    return pl.pallas_call(
        forward_kernel,
        grid_spec=pltpu.PrefetchScalarGridSpec(
            num_scalar_prefetch=2,
            grid=(groups, blocks),
            in_specs=[q_spec, k_spec, v_spec, idq_spec, idk_spec],
            out_specs=[q_spec, lse_spec],
        ),
        out_shape=[
            jax.ShapeDtypeStruct((tok_count, cols), jnp.bfloat16),
            jax.ShapeDtypeStruct((groups, blocks, 128 // HEAD_DIM, query_rows), jnp.float32),
        ],
        compiler_params=pltpu.CompilerParams(vmem_limit_bytes=40 * 1024 * 1024),
        cost_estimate=pl.CostEstimate(
            flops=pairs * 32 * cols, bytes_accessed=2 * qkv.size, transcendentals=2 * pairs
        ),
    )(*bounds, qkv, qkv, qkv, ids_row, ids_col)


def attention_back(qkv, bounds, ids_row, ids_col, att, d_att, lse, group):
    tok_count, cols3 = qkv.shape
    cols = cols3 // 3
    blocks, groups = tok_count // back_rows, cols // 128
    q_spec, k_spec, v_spec, idq_spec, idk_spec, lse_spec = column_specs(
        tok_count, groups, back_rows, group
    )
    pairs = tok_count * tok_count // 2
    out_spec = pl.BlockSpec((back_rows, 128), lambda g, i, *_: (i, 0))
    out_whole = pl.BlockSpec((tok_count, 128), lambda g, i, *_: (0, 0))
    one = jax.ShapeDtypeStruct((tok_count, 128), jnp.bfloat16)
    return pl.pallas_call(
        backward_kernel,
        grid_spec=pltpu.PrefetchScalarGridSpec(
            num_scalar_prefetch=2,
            grid=(1, blocks),
            in_specs=[q_spec, k_spec, v_spec, idq_spec, idk_spec, q_spec, q_spec, lse_spec],
            out_specs=[out_spec, out_whole, out_whole],
            scratch_shapes=[
                pltpu.VMEM((tok_count, 128), jnp.float32),
                pltpu.VMEM((tok_count, 128), jnp.float32),
            ],
        ),
        out_shape=[one, one, one],
        compiler_params=pltpu.CompilerParams(vmem_limit_bytes=48 * 1024 * 1024),
        cost_estimate=pl.CostEstimate(
            flops=pairs * 40 * 128, bytes_accessed=4 * qkv.size, transcendentals=2 * pairs
        ),
    )(*bounds, qkv, qkv, qkv, ids_row, ids_col, att, d_att, lse)


pieces = 2


def entry_kernel(
    outer_count, rest_count, tok_ref, w_in_ref, pack_ref, ids_ref, x_ref, w_ref, packs_ref, ids_out_ref,
    ids_send, ids_recv, ids_sem,
    pack_sem, pack_send, pack_recv, packs_send, packs_recv, move_send, move_recv, rest_send, rest_recv, core_send, core_recv,
    w_send, w_recv, outer_send, outer_recv, own_sem,
):
    o, c, a, r = (lax.axis_index(name) for name in everywhere)
    rows = tok_ref.shape[1]
    part = rows // pieces
    w_rows = w_in_ref.shape[1]
    half, low = a // 2, a % 2
    counts = (outer_count, 2, 4, rest_count)
    here_spot = (o, c, a, r)
    dp_shifts = [(i, j, 0, 0) for i in range(outer_count) for j in range(2)][1:]
    tensor_shifts = [(0, 0, i, j) for i in range(4) for j in range(rest_count)][1:]
    core_shifts = [(0, i, j, 0) for i in range(2) for j in range(4)][1:]

    def away(shift):
        return tuple((spot + s) % n for spot, s, n in zip(here_spot, shift, counts))

    def back(shift):
        return tuple((spot - s + n) % n for spot, s, n in zip(here_spot, shift, counts))

    partners = [away(shift) for shift in sorted({*dp_shifts, *tensor_shifts, *core_shifts})]
    barrier = pltpu.get_barrier_semaphore()
    for partner in partners:
        pl.semaphore_signal(barrier, inc=1, device_id=partner, device_id_type=pl.DeviceIdType.MESH)
    pl.semaphore_wait(barrier, len(partners))
    peer = (o, 1 - c, a, r)

    def remote(src, dst, send, recv, target):
        return pltpu.make_async_remote_copy(
            src_ref=src, dst_ref=dst, send_sem=send, recv_sem=recv,
            device_id=target, device_id_type=pl.DeviceIdType.MESH,
        )

    def pack_spot(spot):
        return packs_ref.at[spot[2] * rest_count + spot[3], spot[0] * 2 + spot[1]]

    def pack_group(spot):
        return packs_ref.at[spot[2] * rest_count + spot[3]]

    def pack_copy(i):
        return remote(
            pack_ref, pack_spot(here_spot), pack_send.at[i], pack_recv.at[i], away(dp_shifts[i])
        )

    def packs_copy(i):
        mine = pack_group(here_spot)
        return remote(mine, mine, packs_send.at[i], packs_recv.at[i], away(tensor_shifts[i]))

    pack_own = pltpu.make_async_copy(pack_ref, pack_spot(here_spot), pack_sem)
    pack_own.start()
    ids_own = pltpu.make_async_copy(ids_ref, ids_out_ref.at[c], ids_sem)
    ids_own.start()
    ids_copy = remote(ids_ref, ids_out_ref.at[c], ids_send, ids_recv, peer)
    ids_copy.start()
    for i in range(len(dp_shifts)):
        pack_copy(i).start()

    def x_rows(seq_spot, rest_spot, piece):
        start = (seq_spot * rest_count + rest_spot) * rows + piece * part
        return x_ref.at[pl.ds(pl.multiple_of(start, part), part), :]

    def tok_rows(batch, piece):
        return tok_ref.at[batch, pl.ds(piece * part, part), :]

    def own_copy(batch, piece):
        return pltpu.make_async_copy(
            tok_rows(batch, piece), x_rows(a, r, piece), own_sem.at[piece]
        )

    def move_copy(batch, piece):
        return remote(
            tok_rows(batch, piece), x_rows(a, r, piece),
            move_send.at[batch, piece], move_recv.at[low, piece], (o, half, 2 * batch + c, r),
        )

    def stays(batch):
        return jnp.logical_and(half == c, 2 * batch + c == a)

    for piece in range(pieces):
        for batch in range(2):
            @pl.when(stays(batch))
            def _():
                own_copy(batch, piece).start()

            @pl.when(jnp.logical_not(stays(batch)))
            def _():
                move_copy(batch, piece).start()

    def w_spot(outer_spot, core_spot, turn):
        start = pl.multiple_of((outer_spot * 2 + core_spot) * w_rows, w_rows)
        return w_ref.at[turn, :, pl.ds(start, w_rows), :]

    w_own = pltpu.make_async_copy(w_in_ref, w_spot(o, c, low), own_sem.at[pieces])

    def w_copy(target):
        return remote(
            w_in_ref, w_spot(o, c, low), w_send.at[target], w_recv.at[c, low], (o, half, target, r)
        )

    for target in range(4):
        same = jnp.logical_and(half == c, a == target)

        @pl.when(same)
        def _():
            w_own.start()

        @pl.when(jnp.logical_not(same))
        def _():
            w_copy(target).start()

    pack_own.wait()
    for i, shift in enumerate(dp_shifts):
        spot = pack_spot(back(shift))
        remote(spot, spot, pack_send.at[i], pack_recv.at[i], peer).wait_recv()
    for i in range(len(tensor_shifts)):
        packs_copy(i).start()

    def rest_copy(turn, piece, shift):
        here = x_rows(2 * c + turn, r, piece)
        return remote(
            here, here, rest_send.at[turn, piece, shift - 1], rest_recv.at[turn, piece, shift - 1],
            (o, c, a, (r + shift) % rest_count),
        )

    def rest_landed(turn, piece, shift):
        here = x_rows(2 * c + turn, (r - shift + rest_count) % rest_count, piece)
        return remote(
            here, here, rest_send.at[turn, piece, shift - 1], rest_recv.at[turn, piece, shift - 1],
            peer,
        )

    def core_copy(turn, piece, shift, core):
        here = x_rows(2 * core + turn, (r - shift + rest_count) % rest_count, piece)
        return remote(
            here, here, core_send.at[turn, piece, shift], core_recv.at[turn, piece, shift], peer
        )

    for piece in range(pieces):
        for turn in range(2):
            same = jnp.logical_and(low == c, 2 * c + turn == a)

            @pl.when(same)
            def _():
                own_copy(0, piece).wait()

            @pl.when(jnp.logical_not(same))
            def _():
                here = x_rows(2 * c + turn, r, piece)
                remote(
                    here, here, move_send.at[0, piece], move_recv.at[turn, piece], peer
                ).wait_recv()

            for shift in range(1, rest_count):
                rest_copy(turn, piece, shift).start()
            core_copy(turn, piece, 0, c).start()

    def outer_copy(core, shift, outer_spot):
        start = pl.multiple_of((outer_spot * 2 + core) * w_rows, w_rows)
        here = w_ref.at[:, :, pl.ds(start, w_rows), :]
        return remote(
            here, here, outer_send.at[core, shift - 1], outer_recv.at[core, shift - 1],
            ((o + shift) % outer_count, c, a, r),
        )

    for core in range(2):
        for turn in range(2):
            same = jnp.logical_and(
                half == c, jnp.logical_and(c == core, low == turn)
            )

            @pl.when(same)
            def _():
                w_own.wait()

            @pl.when(jnp.logical_not(same))
            def _():
                here = w_spot(o, core, turn)
                remote(here, here, w_send.at[0], w_recv.at[core, turn], peer).wait_recv()
        for shift in range(1, outer_count):
            outer_copy(core, shift, o).start()

    for piece in range(pieces):
        for turn in range(2):
            for shift in range(1, rest_count):
                rest_landed(turn, piece, shift).wait_recv()
                core_copy(turn, piece, shift, c).start()

    for core in range(2):
        for shift in range(1, outer_count):
            outer_copy(core, shift, (o - shift + outer_count) % outer_count).wait_recv()
    for piece in range(pieces):
        for turn in range(2):
            for shift in range(rest_count):
                core_copy(turn, piece, shift, 1 - c).wait_recv()

    for piece in range(pieces):
        for batch in range(2):
            @pl.when(jnp.logical_not(stays(batch)))
            def _():
                move_copy(batch, piece).wait_send()
        for turn in range(2):
            for shift in range(1, rest_count):
                rest_copy(turn, piece, shift).wait_send()
            for shift in range(rest_count):
                core_copy(turn, piece, shift, c).wait_send()
    for target in range(4):
        @pl.when(jnp.logical_not(jnp.logical_and(half == c, a == target)))
        def _():
            w_copy(target).wait_send()
    for core in range(2):
        for shift in range(1, outer_count):
            outer_copy(core, shift, o).wait_send()
    for i in range(len(dp_shifts)):
        pack_copy(i).wait_send()
    ids_own.wait()
    ids_copy.wait_send()
    remote(ids_ref, ids_out_ref.at[1 - c], ids_send, ids_recv, peer).wait_recv()
    for i, shift in enumerate(tensor_shifts):
        spot = pack_group(back(shift))
        remote(spot, spot, packs_send.at[i], packs_recv.at[i], peer).wait_recv()
        packs_copy(i).wait_send()


def entry(tokens, qkv_weight, pack, ids):
    outer_count, rest_count = lax.axis_size("o"), lax.axis_size("r")
    batches, rows, width = tokens.shape
    dma = pltpu.SemaphoreType.DMA
    wide, narrow = max(rest_count - 1, 1), max(outer_count - 1, 1)
    return pl.pallas_call(
        lambda *refs: entry_kernel(outer_count, rest_count, *refs),
        in_specs=[pl.BlockSpec(memory_space=pl.ANY)] * 4,
        out_specs=[pl.BlockSpec(memory_space=pl.ANY)] * 4,
        out_shape=[
            jax.ShapeDtypeStruct((4 * rest_count * rows, width), tokens.dtype),
            jax.ShapeDtypeStruct(
                (2, qkv_weight.shape[0], width, qkv_weight.shape[2]), qkv_weight.dtype
            ),
            jax.ShapeDtypeStruct((4 * rest_count, 2 * outer_count, *pack.shape), pack.dtype),
            jax.ShapeDtypeStruct((2, *ids.shape), ids.dtype),
        ],
        scratch_shapes=[
            dma(()), dma(()), dma(()),
            dma(()), dma((2 * outer_count - 1,)), dma((2 * outer_count - 1,)),
            dma((4 * rest_count - 1,)), dma((4 * rest_count - 1,)),
            dma((2, pieces)), dma((2, pieces)),
            dma((2, pieces, wide)), dma((2, pieces, wide)),
            dma((2, pieces, rest_count)), dma((2, pieces, rest_count)),
            dma((4,)), dma((2, 2)), dma((2, narrow)), dma((2, narrow)), dma((pieces + 1,)),
        ],
        compiler_params=pltpu.CompilerParams(collective_id=0, has_side_effects=True),
        cost_estimate=pl.CostEstimate(
            flops=0, bytes_accessed=200 * 1024 * 1024, transcendentals=0
        ),
    )(tokens, qkv_weight, pack, ids)


def tail_kernel(
    outer_count, rest_count, groups, sums_ref, gain_ref, x_ref, d_mid_ref, w_ref, h_ref, mlp_ref,
    proj_ref, *refs,
):
    d_refs, refs = refs[: 3 * groups], refs[3 * groups :]
    total_ref, out_ref, shard_ref, fc1_ref, fc2_ref, proj_out_ref = refs[:6]
    (
        core_buf, core_got, rest_buf, rest_got, own_sum, grad_buf, grad_got, seq_buf, seq_got,
        moved, lines, dp_got, part, tensor_got, proj_got,
        core_send, core_recv, rest_send, rest_recv, grad_send, grad_recv, seq_send, seq_recv,
        seq_own, dp_send, dp_recv, tensor_send, tensor_recv, move_send, move_recv, own_sem,
        proj_send, proj_recv,
    ) = refs[6:]
    o, c, a, r = (lax.axis_index(name) for name in everywhere)
    half, low = a // 2, a % 2
    counts = (outer_count, 2, 4, rest_count)
    here_spot = (o, c, a, r)
    dp_shifts = [(i, j, 0, 0) for i in range(outer_count) for j in range(2)][1:]
    tensor_shifts = [(0, 0, i, j) for i in range(4) for j in range(rest_count)][1:]
    core_shifts = [(0, i, j, 0) for i in range(2) for j in range(4)][1:]

    def away(shift):
        return tuple((spot + s) % n for spot, s, n in zip(here_spot, shift, counts))

    partners = [away(shift) for shift in sorted({*dp_shifts, *tensor_shifts, *core_shifts})]
    barrier = pltpu.get_barrier_semaphore()
    for partner in partners:
        pl.semaphore_signal(barrier, inc=1, device_id=partner, device_id_type=pl.DeviceIdType.MESH)
    pl.semaphore_wait(barrier, len(partners))
    peer = (o, 1 - c, a, r)
    rows = x_ref.shape[1]
    own_cols = 128 * groups
    cols = own_cols // 2
    dp_count = 2 * outer_count
    shard_rows = w_ref.shape[0] // dp_count

    def remote(src, dst, send, recv, target):
        return pltpu.make_async_remote_copy(
            src_ref=src, dst_ref=dst, send_sem=send, recv_sem=recv,
            device_id=target, device_id_type=pl.DeviceIdType.MESH,
        )

    def d_rows(i, spot):
        return jnp.concatenate([d_refs[3 * g + i][spot, :] for g in range(groups)], axis=1)

    def partial(core, turn, shift):
        start = ((2 * core + turn) * rest_count + (r + shift) % rest_count) * rows
        spot = pl.ds(pl.multiple_of(start, rows), rows)
        total = 0.0
        for i in range(3):
            weight = w_ref[:, i * own_cols : (i + 1) * own_cols]
            total = total + dot_f32(d_rows(i, spot), weight, contract_cols)
        return total

    def core_copy(slot):
        return remote(
            core_buf.at[slot], core_got.at[slot], core_send.at[slot], core_recv.at[slot], peer
        )

    def rest_copy(turn, shift):
        return remote(
            rest_buf.at[shift - 1, turn], rest_got.at[shift - 1, turn],
            rest_send.at[shift - 1, turn], rest_recv.at[shift - 1, turn],
            (o, c, a, (r + shift) % rest_count),
        )

    def proj_copy(shift):
        target = (a + shift) % 4
        return remote(
            proj_ref.at[target], proj_got.at[shift - 1], proj_send.at[shift - 1],
            proj_recv.at[shift - 1], (o, c, target, r),
        )

    order = [*range(1, rest_count), 0]
    for shift in order:
        for turn in range(2):
            slot = 2 * shift + turn
            core_buf[slot] = partial(1 - c, turn, shift).astype(jnp.bfloat16)
            core_copy(slot).start()
    for shift in order:
        for turn in range(2):
            slot = 2 * shift + turn
            mine = partial(c, turn, shift)
            core_copy(slot).wait_recv()
            mine = mine + core_got[slot].astype(jnp.float32)
            if shift:
                rest_buf[shift - 1, turn] = mine.astype(jnp.bfloat16)
                rest_copy(turn, shift).start()
            else:
                own_sum[turn] = mine

    for shift in range(1, 4):
        proj_copy(shift).start()

    def grad_copy(shift):
        target = (o + shift) % outer_count
        return remote(
            grad_buf.at[target], grad_got.at[shift - 1], grad_send.at[shift - 1],
            grad_recv.at[shift - 1], (target, c, a, r),
        )

    for d in range(dp_count):
        turned = h_ref[:, d * shard_rows : (d + 1) * shard_rows].T
        for i in range(3):
            grad = dot_f32(turned, d_rows(i, slice(None)))
            grad_buf[d // 2, d % 2, :, i * own_cols : (i + 1) * own_cols] = grad.astype(
                jnp.bfloat16
            )
    for shift in range(1, outer_count):
        grad_copy(shift).start()

    total = 0.0
    for seq in range(4):
        total = total + mlp_ref[seq, 0].astype(jnp.float32)
    fc1_ref[...] = total
    total = 0.0
    for seq in range(4):
        total = total + mlp_ref[seq, 1].astype(jnp.float32)
    fc2_ref[...] = total.T
    total = proj_ref[a].astype(jnp.float32)
    for shift in range(1, 4):
        proj_copy(shift).wait_recv()
        total = total + proj_got[shift - 1].astype(jnp.float32)
    proj_out_ref[...] = total.T

    def stays(turn):
        return jnp.logical_and(low == c, 2 * c + turn == a)

    def move_copy(turn):
        return remote(
            moved.at[turn], out_ref.at[half], move_send.at[turn], move_recv.at[half],
            (o, low, 2 * c + turn, r),
        )

    stay_copy = pltpu.make_async_copy(moved.at[low], out_ref.at[half], own_sem)

    def settle_rows(turn):
        total = own_sum[turn]
        for shift in range(1, rest_count):
            rest_copy(turn, shift).wait_recv()
            total = total + rest_got[shift - 1, turn].astype(jnp.float32)
        normed, rate = norm_parts(x_ref[turn].astype(jnp.float32))
        grad = d_mid_ref[turn] + norm_back(normed, rate, gain_ref[...], total)
        moved[turn] = grad.astype(jnp.bfloat16)

        @pl.when(stays(turn))
        def _():
            stay_copy.start()

        @pl.when(jnp.logical_not(stays(turn)))
        def _():
            move_copy(turn).start()

        gain = jnp.sum(total * normed, axis=0, keepdims=True)
        return gain, jnp.sum(total, axis=0, keepdims=True)

    def mine(block):
        return jnp.logical_and(block // 2 == c, 2 * c + block % 2 == a)

    def seq_copy(block):
        return remote(
            seq_buf.at[block], seq_got.at[a], seq_send.at[block], seq_recv.at[a],
            (o, block // 2, 2 * c + block % 2, r),
        )

    def seq_keep(block):
        return pltpu.make_async_copy(seq_buf.at[block], seq_got.at[a], seq_own)

    first = settle_rows(0)
    for shift in range(1, outer_count):
        grad_copy(shift).wait_recv()
    for core in range(2):
        total = grad_buf[o, core].astype(jnp.float32)
        for shift in range(1, outer_count):
            total = total + grad_got[shift - 1, core].astype(jnp.float32)
        for turn in range(2):
            block = 2 * core + turn
            for i in range(3):
                start = i * own_cols + turn * cols
                seq_buf[block, i] = total[:, start : start + cols].astype(jnp.bfloat16)

            @pl.when(mine(block))
            def _():
                seq_keep(block).start()

            @pl.when(jnp.logical_not(mine(block)))
            def _():
                seq_copy(block).start()
    second = settle_rows(1)

    lines[...] = sums_ref[...]
    for i in range(2):
        line = first[i] + second[i]
        for d in range(dp_count):
            lines[d, i : i + 1, :] = line[:, d * shard_rows : (d + 1) * shard_rows]

    def dp_copy(i):
        target = away(dp_shifts[i])
        return remote(
            lines.at[target[0] * 2 + target[1]], dp_got.at[i], dp_send.at[i], dp_recv.at[i],
            target,
        )

    for i in range(len(dp_shifts)):
        dp_copy(i).start()
    total = lines[o * 2 + c]
    for i in range(len(dp_shifts)):
        dp_copy(i).wait_recv()
        total = total + dp_got[i]
    part[...] = total

    def tensor_copy(i):
        return remote(
            part, tensor_got.at[i], tensor_send.at[i], tensor_recv.at[i], away(tensor_shifts[i])
        )

    for i in range(len(tensor_shifts)):
        tensor_copy(i).start()
    for i in range(len(tensor_shifts)):
        tensor_copy(i).wait_recv()
        total = total + tensor_got[i]
    total_ref[...] = total

    for block in range(4):
        @pl.when(mine(block))
        def _():
            seq_keep(block).wait()
    for seq in range(4):
        here = jnp.logical_and(half == c, a == seq)

        @pl.when(jnp.logical_not(here))
        def _():
            spot = seq_got.at[seq]
            remote(spot, spot, seq_send.at[0], seq_recv.at[seq], peer).wait_recv()
    total = 0.0
    for seq in range(4):
        total = total + seq_got[seq].astype(jnp.float32)
    shard_ref[...] = total

    for batch in range(2):
        same = jnp.logical_and(half == c, 2 * batch + c == a)

        @pl.when(same)
        def _():
            stay_copy.wait()

        @pl.when(jnp.logical_not(same))
        def _():
            spot = out_ref.at[batch]
            remote(spot, spot, move_send.at[0], move_recv.at[batch], peer).wait_recv()
    for turn in range(2):
        @pl.when(jnp.logical_not(stays(turn)))
        def _():
            move_copy(turn).wait_send()
    for block in range(4):
        @pl.when(jnp.logical_not(mine(block)))
        def _():
            seq_copy(block).wait_send()
    for shift in order:
        for turn in range(2):
            core_copy(2 * shift + turn).wait_send()
            if shift:
                rest_copy(turn, shift).wait_send()
    for shift in range(1, outer_count):
        grad_copy(shift).wait_send()
    for shift in range(1, 4):
        proj_copy(shift).wait_send()
    for i in range(len(dp_shifts)):
        dp_copy(i).wait_send()
    for i in range(len(tensor_shifts)):
        tensor_copy(i).wait_send()


def tail(sums, gain, x, d_mid, w_qkv, h, mlp_parts, proj_parts, d_parts):
    outer, rest = lax.axis_size("o"), lax.axis_size("r")
    dma = pltpu.SemaphoreType.DMA
    few, many = 2 * outer - 1, 4 * rest - 1
    wide, narrow = max(rest - 1, 1), max(outer - 1, 1)
    shape = sums.shape[1:]
    _, rows, width = x.shape
    groups = len(d_parts) // 3
    own_cols, shard_rows = 128 * groups, width // (2 * outer)
    low = jnp.bfloat16
    space = pl.BlockSpec(memory_space=pltpu.VMEM)
    return pl.pallas_call(
        lambda *refs: tail_kernel(outer, rest, groups, *refs),
        in_specs=[space] * (8 + 3 * groups),
        out_specs=[space, pl.BlockSpec(memory_space=pl.ANY)] + [space] * 4,
        out_shape=[
            jax.ShapeDtypeStruct(shape, jnp.float32),
            jax.ShapeDtypeStruct(x.shape, low),
            jax.ShapeDtypeStruct((3, shard_rows, own_cols // 2), jnp.float32),
            jax.ShapeDtypeStruct(mlp_parts.shape[2:], jnp.float32),
            jax.ShapeDtypeStruct(mlp_parts.shape[:1:-1], jnp.float32),
            jax.ShapeDtypeStruct(proj_parts.shape[:0:-1], jnp.float32),
        ],
        scratch_shapes=[
            pltpu.VMEM((2 * rest, rows, width), low), pltpu.VMEM((2 * rest, rows, width), low),
            pltpu.VMEM((wide, 2, rows, width), low), pltpu.VMEM((wide, 2, rows, width), low),
            pltpu.VMEM((2, rows, width), jnp.float32),
            pltpu.VMEM((outer, 2, shard_rows, 3 * own_cols), low),
            pltpu.VMEM((narrow, 2, shard_rows, 3 * own_cols), low),
            pltpu.VMEM((4, 3, shard_rows, own_cols // 2), low),
            pltpu.VMEM((4, 3, shard_rows, own_cols // 2), low),
            pltpu.VMEM((2, rows, width), low),
            pltpu.VMEM(sums.shape, jnp.float32),
            pltpu.VMEM((few, *shape), jnp.float32), pltpu.VMEM(shape, jnp.float32),
            pltpu.VMEM((many, *shape), jnp.float32),
            pltpu.VMEM((3, *proj_parts.shape[1:]), low),
            dma((2 * rest,)), dma((2 * rest,)), dma((wide, 2)), dma((wide, 2)),
            dma((narrow,)), dma((narrow,)), dma((4,)), dma((4,)), dma(()),
            dma((few,)), dma((few,)), dma((many,)), dma((many,)), dma((2,)), dma((2,)), dma(()),
            dma((3,)), dma((3,)),
        ],
        compiler_params=pltpu.CompilerParams(
            collective_id=1, has_side_effects=True, vmem_limit_bytes=56 * 1024 * 1024
        ),
        cost_estimate=pl.CostEstimate(
            flops=0, bytes_accessed=250 * 1024 * 1024, transcendentals=0
        ),
    )(sums, gain, x, d_mid, w_qkv, h, mlp_parts, proj_parts, *d_parts)


def mlp_kernel(
    outer_count, rest_count,
    h_ref, dm_ref, w1_ref, w2_ref, bias_ref, m_ref, dh_ref, kept1_ref, got1_ref, kept2_ref,
    got2_ref, dbias_ref, h_turned, dm_turned, kept, sent, got, send_sem, got_sem,
    own_sem, rest_send, rest_recv, outer_send, outer_recv,
):
    o, core, a, r = (lax.axis_index(name) for name in everywhere)
    block = pl.program_id(0)
    count = pl.num_programs(0) - 1
    slot, other = block % 2, (block + 1) % 2
    peer = (o, 1 - core, a, r)
    partners = [peer]
    partners += [(o, core, a, (r + i) % rest_count) for i in range(1, rest_count)]
    partners += [((o + i) % outer_count, core, a, r) for i in range(1, outer_count)]

    def to_rest(index):
        target = index % rest_count
        shift = (target - r + rest_count) % rest_count
        return pltpu.make_async_remote_copy(
            src_ref=got.at[index, 0], dst_ref=got1_ref.at[shift - 1, index // rest_count],
            send_sem=rest_send.at[index], recv_sem=rest_recv.at[shift - 1, index // rest_count],
            device_id=(o, core, a, target), device_id_type=pl.DeviceIdType.MESH,
        )

    def keep_rest(index):
        return pltpu.make_async_copy(
            got.at[index, 0], kept1_ref.at[index // rest_count], own_sem.at[0, index]
        )

    def to_outer(index, shift):
        target = (o + shift) % outer_count
        return pltpu.make_async_remote_copy(
            src_ref=got.at[index, 1, target], dst_ref=got2_ref.at[shift - 1, index],
            send_sem=outer_send.at[shift - 1, index], recv_sem=outer_recv.at[shift - 1, index],
            device_id=(target, core, a, r), device_id_type=pl.DeviceIdType.MESH,
        )

    def keep_outer(index):
        return pltpu.make_async_copy(
            got.at[index, 1, o], kept2_ref.at[index], own_sem.at[1, index]
        )

    def to_peer(index, turn):
        return pltpu.make_async_remote_copy(
            src_ref=sent.at[turn], dst_ref=got.at[index],
            send_sem=send_sem.at[turn], recv_sem=got_sem.at[index],
            device_id=peer, device_id_type=pl.DeviceIdType.MESH,
        )

    @pl.when(block == 0)
    def _():
        barrier = pltpu.get_barrier_semaphore()
        for partner in partners:
            pl.semaphore_signal(
                barrier, inc=1, device_id=partner, device_id_type=pl.DeviceIdType.MESH
            )
        pl.semaphore_wait(barrier, len(partners))
        h_turned[...] = h_ref[...].T
        dm_turned[...] = dm_ref[...].T
        m_ref[...] = jnp.zeros_like(m_ref)
        dh_ref[...] = jnp.zeros_like(dh_ref)

    @pl.when(block >= 2)
    def _():
        to_peer(block - 2, slot).wait_send()

    @pl.when(block < count)
    def _():
        dp_count, _, _, rows = w1_ref.shape
        pre, d_act = bias_ref[...], 0.0
        for d in range(dp_count):
            spot = slice(d * rows, (d + 1) * rows)
            pre = pre + dot_f32(h_ref[:, spot], w1_ref[d, 0], contract_cols)
        for d in range(dp_count):
            spot = slice(d * rows, (d + 1) * rows)
            d_act = d_act + dot_f32(dm_ref[:, spot], w2_ref[d, 0], contract_cols)
        spread = 0.5 * (1.0 + lax.erf(pre * 0.7071067811865476))
        act = (pre * spread).astype(jnp.bfloat16)
        slope = spread + pre * jnp.exp(-0.5 * pre * pre) * 0.3989422804014327
        d_pre = (d_act * slope).astype(jnp.bfloat16)
        dbias_ref[...] = jnp.sum(d_pre.astype(jnp.float32), axis=0, keepdims=True)
        for d in range(dp_count):
            spot = slice(d * rows, (d + 1) * rows)
            m_ref[:, spot] += dot_f32(act, w2_ref[d, 0])
            dh_ref[:, spot] += dot_f32(d_pre, w1_ref[d, 0])
        for d in range(dp_count):
            spot = slice(d * rows, (d + 1) * rows)
            grad1 = dot_f32(h_turned[spot, :], d_pre).astype(jnp.bfloat16)
            grad2 = dot_f32(dm_turned[spot, :], act).astype(jnp.bfloat16)

            @pl.when(core == d % 2)
            def _():
                kept[slot, 0, d // 2] = grad1
                kept[slot, 1, d // 2] = grad2

            @pl.when(core != d % 2)
            def _():
                sent[slot, 0, d // 2] = grad1
                sent[slot, 1, d // 2] = grad2

        to_peer(block, slot).start()

    @pl.when(block >= 1)
    def _():
        to_peer(block - 1, other).wait_recv()
        done = block - 1
        for turn in range(2):
            mine = kept[other, turn].astype(jnp.float32)
            both = mine + got[done, turn].astype(jnp.float32)
            got[done, turn] = both.astype(jnp.bfloat16)

        @pl.when(done % rest_count == r)
        def _():
            keep_rest(done).start()

        @pl.when(done % rest_count != r)
        def _():
            to_rest(done).start()

        keep_outer(done).start()
        for shift in range(1, outer_count):
            to_outer(done, shift).start()

    @pl.when(block == count)
    def _():
        to_peer(block - 1, other).wait_send()

        def settle(index, carry):
            @pl.when(index % rest_count == r)
            def _():
                keep_rest(index).wait()

            @pl.when(index % rest_count != r)
            def _():
                to_rest(index).wait_send()

            keep_outer(index).wait()
            for shift in range(1, outer_count):
                to_outer(index, shift).wait()
            return carry

        lax.fori_loop(0, 4 * rest_count, settle, 0)
        for seq in range(4):
            for shift in range(1, rest_count):
                spot = got1_ref.at[shift - 1, seq]
                pltpu.make_async_remote_copy(
                    src_ref=spot, dst_ref=spot, send_sem=rest_send.at[0],
                    recv_sem=rest_recv.at[shift - 1, seq],
                    device_id=peer, device_id_type=pl.DeviceIdType.MESH,
                ).wait_recv()


def mlp(rows_low, d_branch, weights, hid, bias):
    tokens_here, width = rows_low.shape
    dp_count, tensor_count, _, rows = weights.shape
    outer = dp_count // 2
    whole = pl.BlockSpec((tokens_here, width), lambda t: (0, 0))
    rest = tensor_count // 4
    far = pl.BlockSpec(memory_space=pl.ANY)
    wide, narrow = max(rest - 1, 1), max(outer - 1, 1)
    low = jnp.bfloat16
    dma = pltpu.SemaphoreType.DMA
    out = jax.ShapeDtypeStruct((tokens_here, width), jnp.float32)
    last = tensor_count - 1
    line = pl.BlockSpec((1, hid), lambda t: (0, jnp.minimum(t, last)))
    w1_spec = pl.BlockSpec((dp_count, 1, hid, rows), lambda t: (0, jnp.minimum(t, last), 0, 0))
    w2_spec = pl.BlockSpec((dp_count, 1, hid, rows), lambda t: (0, jnp.minimum(t, last), 1, 0))
    return pl.pallas_call(
        lambda *refs: mlp_kernel(outer, rest, *refs),
        grid=(tensor_count + 1,),
        in_specs=[whole, whole, w1_spec, w2_spec, line],
        out_specs=[whole, whole, far, far, far, far, line],
        out_shape=[
            out, out,
            jax.ShapeDtypeStruct((4, outer, rows, hid), low),
            jax.ShapeDtypeStruct((wide, 4, outer, rows, hid), low),
            jax.ShapeDtypeStruct((tensor_count, rows, hid), low),
            jax.ShapeDtypeStruct((narrow, tensor_count, rows, hid), low),
            jax.ShapeDtypeStruct((1, tensor_count * hid), jnp.float32),
        ],
        scratch_shapes=[
            pltpu.VMEM((width, tokens_here), jnp.bfloat16),
            pltpu.VMEM((width, tokens_here), jnp.bfloat16),
            pltpu.VMEM((2, 2, outer, rows, hid), jnp.bfloat16),
            pltpu.VMEM((2, 2, outer, rows, hid), jnp.bfloat16),
            pltpu.VMEM((tensor_count, 2, outer, rows, hid), jnp.bfloat16),
            dma((2,)), dma((tensor_count,)), dma((2, tensor_count)),
            dma((tensor_count,)), dma((wide, 4)),
            dma((narrow, tensor_count)), dma((narrow, tensor_count)),
        ],
        compiler_params=pltpu.CompilerParams(
            vmem_limit_bytes=60 * 1024 * 1024, collective_id=2, has_side_effects=True
        ),
        cost_estimate=pl.CostEstimate(
            flops=12 * tokens_here * width * tensor_count * hid,
            bytes_accessed=64 * 1024 * 1024,
            transcendentals=2 * tokens_here * tensor_count * hid,
        ),
    )(rows_low, d_branch, weights, weights, bias)


def proj_groups(weights_ref, rest_count):
    for group in range(weights_ref.shape[1] // 2):
        first = 2 * (group // rest_count) * rest_count + group % rest_count
        yield group, first, first + rest_count


def before_kernel(
    rest_count, att_ref, x_ref, dy_ref, weights_ref, vec_ref, mid_ref, branch_ref, h_ref, dm_ref
):
    dp_count, _, depth, rows = weights_ref.shape
    branch = []
    for d in range(dp_count):
        total = vec_ref[2:3, d * rows : (d + 1) * rows]
        for group, one, two in proj_groups(weights_ref, rest_count):
            weight = jnp.concatenate([weights_ref[d, one], weights_ref[d, two]], axis=0)
            total = total + dot_f32(att_ref[group], weight)
        branch.append(total)
    branch = jnp.concatenate(branch, axis=1)
    branch_ref[...] = branch
    middle = x_ref[...].astype(jnp.float32) + vec_ref[3:4] * branch
    mid_ref[...] = middle
    normed, _ = norm_parts(middle)
    h_ref[...] = (normed * vec_ref[4:5] + vec_ref[5:6]).astype(jnp.bfloat16)
    dm_ref[...] = (vec_ref[7:8] * dy_ref[...].astype(jnp.float32)).astype(jnp.bfloat16)


def after_kernel(
    rest_count, m_ref, dh_ref, mid_ref, branch_ref, dy_ref, att_ref, weights_ref, vec_ref,
    out_ref, d_mid_ref, d_att_ref, sums_ref, kept_ref, sent_ref, grad,
):
    step, core = pl.program_id(0), lax.axis_index("c")
    dp_count, _, depth, rows = weights_ref.shape

    @pl.when(step == 0)
    def _():
        sums_ref[...] = jnp.zeros_like(sums_ref)
        grad[...] = jnp.zeros_like(grad)

    middle, dy = mid_ref[...], dy_ref[...].astype(jnp.float32)
    two = m_ref[...] + vec_ref[6:7]
    out_ref[...] = (middle + vec_ref[7:8] * two).astype(jnp.bfloat16)
    dm = (vec_ref[7:8] * dy).astype(jnp.bfloat16).astype(jnp.float32)
    normed, rate = norm_parts(middle)
    d_normed = dh_ref[...]
    d_mid = dy + norm_back(normed, rate, vec_ref[4:5], d_normed)
    d_mid_ref[...] = d_mid
    d_branch = (vec_ref[3:4] * d_mid).astype(jnp.bfloat16)
    lines = [
        d_branch.astype(jnp.float32), d_mid * branch_ref[...], d_normed * normed, d_normed, dm,
        dy * two,
    ]
    for i, line in enumerate(lines):
        sums_ref[i : i + 1] += jnp.sum(line, axis=0, keepdims=True)
    turned = d_branch.T
    for group, one, two in proj_groups(weights_ref, rest_count):
        total = 0.0
        for d in range(dp_count):
            part = slice(d * rows, (d + 1) * rows)
            weight = jnp.concatenate([weights_ref[d, one], weights_ref[d, two]], axis=0)
            total = total + dot_f32(d_branch[:, part], weight, contract_cols)
        d_att_ref[group] = total.astype(jnp.bfloat16)
        both = dot_f32(turned, att_ref[group])
        grad[one] += both[:, :depth]
        grad[two] += both[:, depth:]

    @pl.when(step == pl.num_programs(0) - 1)
    def _():
        for d in range(dp_count):
            part = grad[:, d * rows : (d + 1) * rows].astype(jnp.bfloat16)

            @pl.when(core == d % 2)
            def _():
                kept_ref[:, d // 2] = part

            @pl.when(core != d % 2)
            def _():
                sent_ref[:, d // 2] = part


def side_specs(weights, own_cols, steps, own_rows, width):
    dp_count, tensor_count, total, rows = weights.shape
    depth = own_cols // 2
    tile = own_rows // steps
    groups = tensor_count // 2
    row_spec = pl.BlockSpec((tile, width), lambda i: (i, 0))
    att_spec = pl.BlockSpec((groups, tile, own_cols), lambda i: (0, i, 0))
    w_spec = pl.BlockSpec(
        (dp_count, tensor_count, depth, rows), lambda i: (0, 0, total // depth - 1, 0)
    )
    vec_spec = pl.BlockSpec((8, width), lambda i: (0, 0))
    return row_spec, att_spec, w_spec, vec_spec


side_steps = 2


def before(att, x, dy, weights, vecs):
    own_rows, width = x.shape
    rest = lax.axis_size("r")
    row_spec, att_spec, w_spec, vec_spec = side_specs(
        weights, att.shape[2], side_steps, own_rows, width
    )
    wide = jax.ShapeDtypeStruct((own_rows, width), jnp.float32)
    slim = jax.ShapeDtypeStruct((own_rows, width), jnp.bfloat16)
    return pl.pallas_call(
        lambda *refs: before_kernel(rest, *refs),
        grid=(side_steps,),
        in_specs=[att_spec, row_spec, row_spec, w_spec, vec_spec],
        out_specs=[row_spec] * 4,
        out_shape=[wide, wide, slim, slim],
        compiler_params=pltpu.CompilerParams(vmem_limit_bytes=48 * 1024 * 1024),
        cost_estimate=pl.CostEstimate(
            flops=4 * own_rows * width * width, bytes_accessed=16 * 1024 * 1024, transcendentals=0
        ),
    )(att, x, dy, weights, vecs)


def after(m, dh, middle, branch, dy, att, weights, vecs):
    own_rows, width = m.shape
    rest, outer = lax.axis_size("r"), lax.axis_size("o")
    tensor_count, rows = weights.shape[1], weights.shape[3]
    depth = att.shape[2] // 2
    row_spec, att_spec, w_spec, vec_spec = side_specs(
        weights, att.shape[2], side_steps, own_rows, width
    )
    grad_spec = pl.BlockSpec((tensor_count, outer, rows, depth), lambda i: (0, 0, 0, 0))
    grad = jax.ShapeDtypeStruct((tensor_count, outer, rows, depth), jnp.bfloat16)
    return pl.pallas_call(
        lambda *refs: after_kernel(rest, *refs),
        grid=(side_steps,),
        in_specs=[row_spec] * 5 + [att_spec, w_spec, vec_spec],
        out_specs=[row_spec, row_spec, att_spec, vec_spec, grad_spec, grad_spec],
        out_shape=[
            jax.ShapeDtypeStruct((own_rows, width), jnp.bfloat16),
            jax.ShapeDtypeStruct((own_rows, width), jnp.float32),
            jax.ShapeDtypeStruct(att.shape, jnp.bfloat16),
            jax.ShapeDtypeStruct((8, width), jnp.float32),
            grad, grad,
        ],
        scratch_shapes=[pltpu.VMEM((tensor_count, width, depth), jnp.float32)],
        compiler_params=pltpu.CompilerParams(vmem_limit_bytes=56 * 1024 * 1024),
        cost_estimate=pl.CostEstimate(
            flops=8 * own_rows * width * width, bytes_accessed=24 * 1024 * 1024, transcendentals=0
        ),
    )(m, dh, middle, branch, dy, att, weights, vecs)


def gather_parts(shard):
    parts = lax.all_gather(shard, everywhere, axis=0, tiled=False)
    return parts.reshape(lax.axis_size("o") * 2, -1, *shard.shape)


def pick(blocks, index):
    return lax.dynamic_index_in_dim(blocks, index, 0, keepdims=False)


def place_shift(step, count):
    return [(spot, (spot + step) % count) for spot in range(count)]


def move_pairs(step):
    pairs = []
    for core in range(2):
        for seq in range(4):
            batch = (seq % 2) ^ step
            pairs.append((core * 4 + seq, (seq // 2) * 4 + 2 * batch + core))
    return pairs


def move_in(both):
    low = lax.axis_index("a") % 2
    batch = lax.axis_index("a") // 2
    got = [
        lax.ppermute(pick(both, low ^ step), ("c", "a"), move_pairs(step)) for step in range(2)
    ]
    return jnp.stack([jnp.where(batch == 0, got[j], got[1 - j]) for j in range(2)])


def move_out(own):
    low = lax.axis_index("a") % 2
    batch = lax.axis_index("a") // 2
    got = [
        lax.ppermute(
            pick(own, batch ^ step), ("c", "a"), [(t, s) for s, t in move_pairs(step)]
        )
        for step in range(2)
    ]
    return jnp.stack([jnp.where(low == 0, got[b], got[1 - b]) for b in range(2)])


def sum_shards(blocks, axis, dim, dtype):
    count, me = blocks.shape[dim], lax.axis_index(axis)

    def block(spot):
        return lax.dynamic_index_in_dim(blocks, spot, dim, keepdims=False)

    got = [
        lax.ppermute(block((me + step) % count), axis, place_shift(step, count))
        for step in range(1, count)
    ]
    total = block(me).astype(jnp.float32)
    for values in got:
        total = total + values.astype(jnp.float32)
    return total.astype(dtype)


def seq_parts(blocks):
    me = lax.axis_index("a")
    parts = [pick(blocks, me)]
    for step in range(1, 4):
        parts.append(lax.ppermute(pick(blocks, (me + step) % 4), "a", place_shift(step, 4)))
    return parts


def pair_sum(kept, got, count):
    total = kept.astype(jnp.float32)
    for i in range(count):
        total = total + got[i].astype(jnp.float32)
    return total.astype(jnp.bfloat16)


def core_sum(own, sent):
    got = lax.ppermute(sent, "c", [(0, 1), (1, 0)])
    total = (own.astype(jnp.float32) + got.astype(jnp.float32)).astype(jnp.bfloat16)
    return total.reshape(4, lax.axis_size("r"), *total.shape[1:])


def body(
    tokens, segment_ids, out_grad, norm1_gain, norm1_bias, qkv_weight, qv_bias, proj_weight,
    proj_bias, scale1, norm2_gain, norm2_bias, fc1_weight, fc1_bias, fc2_weight, fc2_bias, scale2,
):
    o, c, a, r = (lax.axis_index(name) for name in everywhere)
    outer, rest = lax.axis_size("o"), lax.axis_size("r")
    dp_count, tensor_count = outer * 2, 4 * rest
    batches, rows_here, width = tokens.shape
    own_rows = 2 * rows_here
    tok_count = rows_here * tensor_count
    cols_here, shard_rows = qkv_weight.shape[2], qkv_weight.shape[1]
    own_cols = 2 * cols_here
    hidden = fc1_weight.shape[1] * tensor_count
    short, fc1_short = qv_bias.shape[1], fc1_bias.shape[0]

    vectors = jnp.stack(
        [norm1_gain, norm1_bias, proj_bias, scale1, norm2_gain, norm2_bias, fc2_bias, scale2]
    )
    small = jnp.concatenate([qv_bias.reshape(-1), fc1_bias])
    small = jnp.pad(small[None], ((0, 7), (0, shard_rows - small.shape[0])))
    seq_rows, w_parts, packs, ids = entry(
        tokens, qkv_weight, jnp.concatenate([vectors, small]), segment_ids
    )
    seq_rows, out_grad = lax.optimization_barrier((seq_rows, out_grad))
    vecs = jnp.moveaxis(packs[0, :, :8], 0, 1).reshape(8, width).astype(jnp.float32)
    biases = packs[:, :, 8].astype(jnp.float32)
    bias_fc1 = biases[:, :, 2 * short : 2 * short + fc1_short].reshape(hidden)
    bias_qv = biases[:, :, : 2 * short].reshape(2, 2, rest, dp_count, 2, short)
    bias_qv = lax.dynamic_index_in_dim(bias_qv, c, 0, keepdims=False)
    bias_qv = lax.dynamic_index_in_dim(bias_qv, r, 1, keepdims=False)
    bias_qv = jnp.moveaxis(bias_qv, 2, 0).reshape(2, own_cols)
    bias_qkv = jnp.concatenate([bias_qv[0], jnp.zeros_like(bias_qv[0]), bias_qv[1]])
    scale_qkv = jnp.concatenate([jnp.full((own_cols,), 0.125), jnp.ones((2 * own_cols,))])

    run_ids = pick(pick(ids, a % 2), a // 2)[0]

    def key_bounds(rows):
        split = run_ids.reshape(tok_count // rows, rows)
        low = jnp.sum((run_ids[None] < split[:, :1]).astype(jnp.int32), axis=-1) // key_rows
        reach = jnp.sum((run_ids[None] <= split[:, -1:]).astype(jnp.int32), axis=-1)
        return low, (reach + key_rows - 1) // key_rows

    bounds, back_bounds = key_bounds(query_rows), key_bounds(back_rows)
    ids_row, ids_col = run_ids[None, :], run_ids[:, None]

    weights = gather_parts(jnp.concatenate([fc1_weight.T, fc2_weight, proj_weight]))
    w_qkv = jnp.moveaxis(w_parts, 0, 2).swapaxes(0, 1).reshape(width, 3 * own_cols)

    def own_of(values):
        split = values.reshape(2, 2, rest, rows_here, values.shape[1])
        split = lax.dynamic_index_in_dim(split, c, 0, keepdims=False)
        split = lax.dynamic_index_in_dim(split, r, 1, keepdims=False)
        return split.reshape(own_rows, values.shape[1])

    normed_all, _ = norm_parts(seq_rows.astype(jnp.float32))
    normed_all_low = (normed_all * vecs[0] + vecs[1]).astype(jnp.bfloat16)
    qkv = ((dot_f32(normed_all_low, w_qkv) + bias_qkv) * scale_qkv).astype(jnp.bfloat16)
    grad_moved = move_in(out_grad)
    att_heads, lse = attention(qkv, bounds, ids_row, ids_col)
    lse = lse.reshape(*lse.shape[:3], query_rows // back_rows, back_rows)
    lse = jnp.swapaxes(lse, 2, 3).reshape(lse.shape[0], -1, lse.shape[2], back_rows)

    rows_own = own_of(seq_rows)
    grad_top = grad_moved.reshape(own_rows, width)
    sent = att_heads.reshape(2, 2, rest, rows_here, own_cols)
    sent = jnp.swapaxes(sent, 1, 2).reshape(2 * rest, own_rows, own_cols)
    attended = lax.all_to_all(sent, ("c", "r"), split_axis=0, concat_axis=0, tiled=True)
    middle, branch_one, mlp_in, d_branch2 = before(attended, rows_own, grad_top, weights, vecs)
    branch_two, d_normed_two, kept1, got1, kept2, got2, d_fc1_bias = mlp(
        mlp_in, d_branch2, weights, fc2_weight.shape[0], bias_fc1[None]
    )
    grad_fc1 = pair_sum(kept1, got1, rest - 1)
    grad_fc2 = pair_sum(kept2, got2, outer - 1).reshape(4, rest, *kept2.shape[1:])
    branch_two, grad_fc1, grad_fc2 = lax.optimization_barrier((branch_two, grad_fc1, grad_fc2))
    grad_fc1 = sum_shards(grad_fc1, "o", 1, jnp.bfloat16)
    grad_fc2 = sum_shards(grad_fc2, "r", 1, jnp.bfloat16)
    block_out, d_middle, sent, line_sums, proj_kept, proj_sent = after(
        branch_two, d_normed_two, middle, branch_one, grad_top, attended, weights, vecs
    )
    d_heads = lax.all_to_all(sent, ("c", "r"), split_axis=0, concat_axis=0, tiled=True)
    d_heads = jnp.swapaxes(d_heads.reshape(2, rest, 2, rows_here, own_cols), 1, 2)
    d_heads = d_heads.reshape(tok_count, own_cols)
    grad_proj = core_sum(proj_kept, proj_sent)
    d_heads, grad_fc1, grad_fc2, grad_proj, block_out = lax.optimization_barrier(
        (d_heads, grad_fc1, grad_fc2, grad_proj, block_out)
    )

    block_out = move_out(block_out.reshape(2, rows_here, width))
    mlp_parts = jnp.stack([grad_fc1, grad_fc2], axis=1)
    mlp_parts = lax.all_to_all(mlp_parts, "a", split_axis=0, concat_axis=0, tiled=True)
    grad_proj = sum_shards(grad_proj, "o", 2, jnp.bfloat16)
    groups = own_cols // 128
    d_parts = []
    for group in range(groups):
        d_parts.append(
            attention_back(qkv, back_bounds, ids_row, ids_col, att_heads, d_heads, lse, group)
        )
        if group == 0:
            d_parts, d_heads, grad_proj = lax.optimization_barrier((d_parts, d_heads, grad_proj))
            grad_proj = sum_shards(grad_proj, "r", 1, jnp.bfloat16)
    d_parts, grad_proj, block_out, mlp_parts = lax.optimization_barrier(
        (d_parts, grad_proj, block_out, mlp_parts)
    )
    d_bias_qv = jnp.stack(
        [
            jnp.concatenate([jnp.sum(part[i].astype(jnp.float32), axis=0) for part in d_parts])
            for i in (0, 2)
        ]
    ).reshape(2, 2, cols_here)
    spread_qv = jnp.zeros((2, 2, 2, rest, cols_here), jnp.float32)
    spread_qv = lax.dynamic_update_slice(
        spread_qv, d_bias_qv[:, None, :, None], (0, c, 0, r, 0)
    )
    lines = jnp.concatenate([line_sums[6:], line_sums[:6]]).reshape(8, dp_count, shard_rows)
    fc1_lines = d_fc1_bias.reshape(tensor_count, dp_count, fc1_short)
    fc1_lines = jnp.swapaxes(fc1_lines, 0, 1).reshape(dp_count, -1, shard_rows)
    qv_lines = spread_qv.reshape(2, tensor_count, dp_count, short)
    qv_lines = jnp.moveaxis(qv_lines, 2, 0).reshape(dp_count, -1, shard_rows)
    sums = jnp.concatenate([jnp.swapaxes(lines, 0, 1), fc1_lines, qv_lines], axis=1)
    sums = jnp.pad(sums, ((0, 0), (0, -sums.shape[1] % 8), (0, 0)))
    vec_sums, input_grad, shard_qkv, shard_fc1, shard_fc2, shard_proj = tail(
        sums, vecs[:1], rows_own.reshape(2, rows_here, width),
        d_middle.reshape(2, rows_here, width), w_qkv, normed_all_low, mlp_parts, grad_proj,
        [values for part in d_parts for values in part],
    )
    place = a * rest + r
    fc1_rows = fc1_lines.shape[1]
    grad_fc1_bias = vec_sums[8 : 8 + fc1_rows].reshape(tensor_count, fc1_short)
    grad_fc1_bias = pick(grad_fc1_bias, place)
    grad_qv_bias = vec_sums[8 + fc1_rows : 8 + fc1_rows + qv_lines.shape[1]]
    grad_qv_bias = lax.dynamic_index_in_dim(
        grad_qv_bias.reshape(2, tensor_count, short), place, 1, keepdims=False
    )
    return (
        block_out,
        input_grad,
        vec_sums[0],
        vec_sums[1],
        shard_qkv,
        grad_qv_bias,
        shard_proj,
        vec_sums[2],
        vec_sums[3],
        vec_sums[4],
        vec_sums[5],
        shard_fc1,
        grad_fc1_bias,
        shard_fc2,
        vec_sums[6],
        vec_sums[7],
    )


def solution(mesh):
    dp, tensor = ("o", "c"), ("a", "r")
    dp_count, tensor_count = mesh.devices.shape
    finer = Mesh(mesh.devices.reshape(dp_count // 2, 2, 4, tensor_count // 4), everywhere)
    rows = P(None, everywhere, None)
    vec = P(dp)
    in_specs = (
        rows, P(None, dp, None), rows, vec, vec, P(None, dp, tensor), P(None, tensor + dp),
        P(tensor, dp), vec, vec, vec, vec, P(dp, tensor), P(tensor + dp), P(tensor, dp), vec, vec,
    )
    out_specs = (
        rows, rows, vec, vec, P(None, dp, tensor), P(None, tensor + dp), P(tensor, dp), vec, vec,
        vec, vec, P(dp, tensor), P(tensor + dp), P(tensor, dp), vec, vec,
    )
    return jax.shard_map(body, mesh=finer, in_specs=in_specs, out_specs=out_specs, check_vma=False)
```
